512 devices in a mesh: seg: 16 (over y, x_hi), grp: 32 (over z, x_lo, core).
Axes of the slice: x: 4 (x_hi: 2, x_lo: 2; x = x_hi * 2 + x_lo), y: 8, z: 8, core: 2. Of those that a mesh axis runs over, the one named last changes fastest.
Arguments:
- queries: bfloat16 [20480, 2048], P(('seg', 'grp')), may hold values from -8 to 8
- keys: bfloat16 [20480, 2048], P(('seg', 'grp')), may hold values from -8 to 8
- values: bfloat16 [20480, 2048], P(('seg', 'grp')), may hold values from -6 to 6
- rates: bfloat16 [20480, 32], P(('seg', 'grp')), may hold values from 0 to 0.45
- text_valid: int32 [16], P('seg'), may hold values from 32 to 128, as said below
- state_fwd: float32 [32, 64, 64], P('grp'), may hold values from -0.75 to 0.75
- state_bwd: float32 [32, 64, 64], P('grp'), may hold values from -0.75 to 0.75
Outputs:
- mixed: bfloat16 [20480, 2048], P(('seg', 'grp'))
The draws below stay inside these ranges and needn't reach their ends.
Inputs may be any that keep to these rules, and one draw needn't show every extreme that they name: `text_valid`: the number of valid text tokens among the first 128 positions of each segment.
All inputs are finite; a program needn't handle non-finite values.
Results may differ from the reference program's by a relative error of at most 0.0045.
Values may be sent and summed in bfloat16 or wider, within the bound.
No kernel may reach another device: no remote copies, remote signals or barrier semaphores. Data moves between devices by JAX's collectives and lax.ppermute only.
A program may use at most 64 MiB of HBM per device.

```python
import math
import jax
import jax.numpy as jnp
from jax import lax

ACTIVE_HEADS = 32
HDIM = 64
GROUP = 64
TEXT = 128
SEGLEN = 1280
CLIP_TOKENS = 20480
WIDTH = 2048
N_SEG = 16


def draw_queries(key, part):
    key = jax.random.fold_in(key, 1)
    value_field = jnp.clip(1.7 * jax.random.normal(key, (CLIP_TOKENS, WIDTH), jnp.float32), -8.0, 8.0)
    return value_field.astype(jnp.bfloat16)


def draw_keys(key, part):
    key = jax.random.fold_in(key, 2)
    value_field = jnp.clip(1.7 * jax.random.normal(key, (CLIP_TOKENS, WIDTH), jnp.float32), -8.0, 8.0)
    return value_field.astype(jnp.bfloat16)


def draw_rates(key, part):
    key = jax.random.fold_in(key, 3)
    random_subkeys = jax.random.split(key, 7)
    block_count = CLIP_TOKENS // GROUP
    segments = CLIP_TOKENS // SEGLEN
    quick_share = 0.5
    quick_heads = jax.random.uniform(random_subkeys[0], (ACTIVE_HEADS,), jnp.float32) < quick_share
    quick_rate = jnp.exp(jax.random.uniform(random_subkeys[1], (ACTIVE_HEADS,), jnp.float32, math.log(0.06), math.log(0.2)))
    steady_rate = jnp.exp(jax.random.uniform(random_subkeys[2], (ACTIVE_HEADS,), jnp.float32, math.log(0.25), math.log(0.8))) / block_count
    base_rate = jnp.where(quick_heads, quick_rate, steady_rate)
    segment_factor = jnp.exp(jax.random.uniform(random_subkeys[3], (segments, 1, ACTIVE_HEADS), jnp.float32, math.log(0.7), math.log(1.4)))
    token_multiplier = jax.random.uniform(random_subkeys[4], (segments, SEGLEN, ACTIVE_HEADS), jnp.float32, 0.5, 1.5)
    value_field = (base_rate[None, None, :] * segment_factor * token_multiplier).reshape(CLIP_TOKENS, ACTIVE_HEADS)
    spike_runs = jax.random.randint(random_subkeys[5], (2,), 0, block_count)
    owning_block = jnp.arange(CLIP_TOKENS) // GROUP
    inside_spike = jnp.any(owning_block[:, None] == spike_runs[None, :], axis=1)
    spike_rate = jax.random.uniform(random_subkeys[6], (ACTIVE_HEADS,), jnp.float32, 0.2, 0.3)
    value_field = jnp.where(inside_spike[:, None], spike_rate[None, :] * token_multiplier.reshape(CLIP_TOKENS, ACTIVE_HEADS), value_field)
    return value_field.astype(jnp.bfloat16)


def draw_text_valid(key, part):
    key = jax.random.fold_in(key, 5)
    random_subkeys = jax.random.split(key, 2)
    segments = CLIP_TOKENS // SEGLEN
    lengths = jax.random.randint(random_subkeys[0], (segments,), TEXT // 4, TEXT + 1)
    order = jax.random.permutation(random_subkeys[1], segments)
    lengths = lengths.at[order[0]].set(TEXT).at[order[1]].set(TEXT // 4)
    return lengths.astype(jnp.int32)


def steps_of(stream_key, extent, cuts, least, top_value):
    def one(dim, parts):
        draws = jax.random.uniform(jax.random.fold_in(jax.random.fold_in(stream_key, 6), dim), (parts,), jnp.float32, least / len(cuts), top_value / len(cuts))
        return jnp.repeat(jnp.exp(draws), extent[dim] // parts).reshape((-1,) + (1,) * (len(extent) - dim - 1))

    gain = one(*cuts[0])
    for cut in cuts[1:]:
        gain = gain * one(*cut)
    return gain


def centred(stream_key, extent, deviation, most, pieces=(), kind=jnp.bfloat16):
    drawn = deviation * jax.random.normal(stream_key, extent, jnp.float32)
    if pieces:
        drawn = drawn * steps_of(stream_key, extent, pieces, -0.22, 0.18)
    return jnp.clip(drawn, -most, most).astype(kind)


def setup_inputs(seed: int = 0) -> dict:
    splits = jax.random.split(jax.random.key(seed), 8)
    queries = draw_queries(jax.random.fold_in(splits[7], 71), 0)
    keys = draw_keys(jax.random.fold_in(splits[7], 71), 0)
    values = centred(splits[2], (CLIP_TOKENS, WIDTH), 1.0, 6.0, ((0, 512),))
    rates = draw_rates(jax.random.fold_in(splits[7], 71), 0)
    text_valid = draw_text_valid(jax.random.fold_in(splits[7], 71), 0)
    state_fwd = centred(splits[5], (ACTIVE_HEADS, HDIM, HDIM), HDIM ** -0.5, 0.75, ((0, 32),), jnp.float32)
    state_bwd = centred(splits[6], (ACTIVE_HEADS, HDIM, HDIM), HDIM ** -0.5, 0.75, ((0, 32),), jnp.float32)
    return {"queries": queries, "keys": keys, "values": values, "rates": rates, "text_valid": text_valid, "state_fwd": state_fwd, "state_bwd": state_bwd}


precise = lax.Precision.HIGHEST

def unit_rows(features):
    return features * lax.rsqrt(lax.optimization_barrier(jnp.sum(features * features, axis=-1, keepdims=True)) + 1e-06)

def attend_head(query_rows, key_rows, value_rows, live_keys):
    scaling = 1.0 / math.sqrt(HDIM)
    block_rows = math.gcd(512, SEGLEN)

    def one_block(query_block):
        scores = jnp.dot(query_block, key_rows.T, preferred_element_type=jnp.float32) * scaling
        scores = jnp.where(live_keys[None, :], scores, -1e+30)
        row_peak = lax.optimization_barrier(jnp.max(scores, axis=1, keepdims=True))
        raised = jnp.exp(scores - row_peak)
        row_total = lax.optimization_barrier(jnp.sum(raised, axis=1, keepdims=True))
        weights = raised.astype(jnp.bfloat16)
        gathered = jnp.dot(weights, value_rows, preferred_element_type=jnp.float32)
        return (gathered / row_total).astype(jnp.bfloat16)
    blocks = lax.map(one_block, query_rows.reshape(SEGLEN // block_rows, block_rows, HDIM))
    return blocks.reshape(SEGLEN, HDIM)

def inner_pass(unit_queries, unit_keys, targets, rate_live, start):
    lower = (jnp.arange(GROUP)[:, None] >= jnp.arange(GROUP)[None, :]).astype(jnp.float32)
    blocks = CLIP_TOKENS // GROUP

    def one_step(state, block):
        block_q, block_k, block_v, block_r = block
        resid = jnp.einsum('thd,hde->the', block_k, state, precision=precise) - block_v
        grad = block_r[:, :, None] * resid
        inner = jnp.einsum('thd,shd->hts', block_q, block_k, precision=precise) * lower[None]
        result = jnp.einsum('thd,hde->the', block_q, state, precision=precise) - jnp.einsum('hts,she->the', inner, grad, precision=precise)
        state = state - jnp.einsum('thd,the->hde', block_k, grad, precision=precise)
        return (state, result)

    def as_blocks(array):
        return array.reshape((blocks, GROUP) + array.shape[1:])
    final_state, results = lax.scan(one_step, start, (as_blocks(unit_queries), as_blocks(unit_keys), as_blocks(targets), as_blocks(rate_live)))
    return results.reshape(CLIP_TOKENS, ACTIVE_HEADS, HDIM)

def by_head(array):
    return array.reshape(N_SEG, SEGLEN, ACTIVE_HEADS, HDIM).transpose(0, 2, 1, 3)

def reference(queries, keys, values, rates, text_valid, state_fwd, state_bwd):
    position = jnp.arange(SEGLEN)
    live = (position[None, :] >= TEXT) | (position[None, :] < text_valid[:, None])

    def one_segment(inputs):
        seg_q, seg_k, seg_v, seg_live = inputs

        def one_head(triple):
            return attend_head(triple[0], triple[1], triple[2], seg_live)
        return lax.map(one_head, (seg_q, seg_k, seg_v))
    attended = lax.map(one_segment, (by_head(queries), by_head(keys), by_head(values), live))
    attended = attended.transpose(0, 2, 1, 3).reshape(CLIP_TOKENS, ACTIVE_HEADS, HDIM)
    live_tokens = live.reshape(CLIP_TOKENS).astype(jnp.float32)
    rate_live = rates.astype(jnp.float32) * live_tokens[:, None]
    unit_queries = math.sqrt(HDIM) * unit_rows(queries.astype(jnp.float32).reshape(CLIP_TOKENS, ACTIVE_HEADS, HDIM))
    unit_keys = unit_rows(keys.astype(jnp.float32).reshape(CLIP_TOKENS, ACTIVE_HEADS, HDIM))
    targets = attended.astype(jnp.float32)
    forward = inner_pass(unit_queries, unit_keys, targets, rate_live, state_fwd)
    backward = inner_pass(unit_queries[::-1], unit_keys[::-1], targets[::-1], rate_live[::-1], state_bwd)[::-1]
    mixed = targets + forward + backward
    return mixed.reshape(CLIP_TOKENS, ACTIVE_HEADS * HDIM).astype(jnp.bfloat16)
```

```python
import functools
import math

import jax
import jax.numpy as jnp
from jax import lax
from jax.experimental import pallas as pl
from jax.experimental.pallas import tpu as pltpu
from jax.sharding import PartitionSpec as P

GROUP = 64
TEXT = 128
HDIM = 64
LANES = 128
QROWS = 256
VMEM_LIMIT = 48 * 1024 * 1024

bf16 = jnp.bfloat16
f32 = jnp.float32


def split(x):
    hi = x.astype(bf16)
    return hi, (x - hi.astype(f32)).astype(bf16)


def mm(a, b):
    return lax.dot_general(a, b, (((1,), (0,)), ((), ())), preferred_element_type=f32)


def mm_nt(a, b):
    return lax.dot_general(a, b, (((1,), (1,)), ((), ())), preferred_element_type=f32)


def mm_tn(a, b):
    return lax.dot_general(a, b, (((0,), (0,)), ((), ())), preferred_element_type=f32)


def mm3(a, b):
    a_hi, a_lo = split(a)
    b_hi, b_lo = split(b)
    return mm(jnp.concatenate([a_hi, a_lo, a_hi], axis=1), jnp.concatenate([b_hi, b_hi, b_lo], axis=0))


def lanes_left(rows):
    return lax.broadcasted_iota(jnp.int32, (rows, LANES), 1) < HDIM


def swap_halves(x):
    return pltpu.roll(x, HDIM, 1)


def pack_body(q_ref, k_ref, v_ref, r_ref, o_ref, rate_scr):
    rows, width = q_ref.shape
    heads = width // HDIM
    late = rows - 24
    left = lanes_left(rows)
    left24 = lanes_left(24)
    rate_scr[...] = jnp.zeros_like(rate_scr)
    rate_scr[:, 0:rows] = r_ref[...].astype(f32)
    for p in range(heads // 2):
        cols = slice(LANES * p, LANES * (p + 1))
        q = q_ref[:, cols].astype(f32)
        k = k_ref[:, cols].astype(f32)
        v = v_ref[:, cols].astype(f32)
        q_sw, k_sw, v_sw = swap_halves(q), swap_halves(k), swap_halves(v)
        for odd in (0, 1):
            head = 2 * p + odd
            qk = jnp.where(left, q_sw, k) if odd else jnp.where(left, q, k_sw)
            v_right, v_left = (v, v_sw) if odd else (v_sw, v)
            rate = jnp.broadcast_to(rate_scr[head : head + 1, :], (24 - late, LANES))
            low = jnp.concatenate([v_left[24:rows], rate], axis=0)
            vr = jnp.where(left24, low, v_right[0:24])
            o_ref[head] = jnp.concatenate([qk, vr], axis=0).astype(bf16)


def pack(queries, keys, values, rates_t):
    rows, width = queries.shape
    heads = width // HDIM
    return pl.pallas_call(
        pack_body,
        out_shape=jax.ShapeDtypeStruct((heads, rows + 24, LANES), bf16),
        scratch_shapes=[pltpu.VMEM((heads, LANES), f32)],
        compiler_params=pltpu.CompilerParams(vmem_limit_bytes=VMEM_LIMIT),
        name="pack",
    )(queries, keys, values, rates_t)


def attend_body(
    tv_ref, me_ref, recv_ref, msg_ref, xf_ref, xb_ref, kq_ref, yhi_ref, ylo_ref, att_ref, sq_ref,
    qk_scr, v_scr, r_scr,
):
    groups, rows, _ = recv_ref.shape
    toks = rows - 24
    late = toks - 24
    seglen = groups * toks
    chunks = seglen // GROUP
    valid = tv_ref[0]
    me = me_ref[0]

    pick = lax.broadcasted_iota(jnp.int32, (toks, LANES), 0) == lax.broadcasted_iota(jnp.int32, (toks, LANES), 1)
    for g in range(groups):
        block = recv_ref[g].astype(f32)
        base = toks * g
        qk_scr[base : base + toks] = block[0:toks]
        v_scr[base : base + 24] = block[toks : toks + 24]
        v_scr[base + 24 : base + toks] = swap_halves(block[toks : toks + late])
        r_scr[base : base + toks] = jnp.where(pick, block[toks + late : toks + late + 1], 0.0)

    v_all = v_scr[...].astype(bf16)
    kq_all = swap_halves(qk_scr[...]).astype(bf16)
    kq_ref[...] = kq_all

    row_id = lax.broadcasted_iota(jnp.int32, (2 * LANES, 2 * LANES), 0)
    col_id = lax.broadcasted_iota(jnp.int32, (2 * LANES, 2 * LANES), 1)
    is_key_row = lax.rem(row_id, LANES) >= HDIM
    sums = jnp.where(is_key_row == (col_id < LANES), 1.0, 0.0).astype(bf16)
    ones = jnp.ones((LANES, LANES), bf16)
    left = lanes_left(QROWS)
    cols = lax.broadcasted_iota(jnp.int32, (QROWS, TEXT), 1)

    for b in range(seglen // QROWS):
        at = slice(QROWS * b, QROWS * (b + 1))
        qk = qk_scr[at]
        squares_hi, squares_lo = split(qk * qk)
        total = mm(jnp.concatenate([squares_hi, squares_lo], axis=1), sums)
        inv = lax.rsqrt(total + 1e-06)
        inv_k = inv[:, 0:LANES]
        sq_ref[at] = math.sqrt(HDIM) * inv[:, LANES : 2 * LANES]
        rate = mm(r_scr[at].astype(bf16), ones)
        if QROWS * b < TEXT:
            position = QROWS * b + lax.broadcasted_iota(jnp.int32, (QROWS, LANES), 0)
            rate = jnp.where((position >= TEXT) | (position < valid), rate, 0.0)
        q_scaled = jnp.where(left, qk * (1.0 / math.sqrt(HDIM)), 0.0).astype(bf16)
        scores = mm_nt(q_scaled, kq_all)
        head_part = jnp.where(cols < valid, scores[:, 0:TEXT], -1e30)
        scores = jnp.concatenate([head_part, scores[:, TEXT:]], axis=1)
        peak = jnp.max(scores, axis=1, keepdims=True)
        raised = jnp.exp(scores - peak)
        row_total = jnp.sum(raised, axis=1, keepdims=True)
        gathered = mm(raised.astype(bf16), v_all)
        att = (gathered / row_total).astype(bf16)
        att_ref[at] = att
        step = rate * inv_k
        y = jnp.where(left, step * inv_k * swap_halves(qk), step * att.astype(f32))
        y_hi, y_lo = split(y)
        yhi_ref[at] = y_hi
        ylo_ref[at] = y_lo

    maps = []
    for n in range(chunks):
        at = slice(GROUP * n, GROUP * (n + 1))
        k = kq_ref[at, 0:HDIM]
        maps.append(mm_tn(jnp.concatenate([k, k], axis=0), jnp.concatenate([yhi_ref[at], ylo_ref[at]], axis=0)))

    left64 = lanes_left(HDIM)
    eye = jnp.where(
        lax.broadcasted_iota(jnp.int32, (HDIM, LANES), 0) == lax.broadcasted_iota(jnp.int32, (HDIM, LANES), 1), 1.0, 0.0
    )

    def advance(x, gb):
        return x - mm3(gb[:, 0:HDIM], x) + jnp.where(left64, 0.0, gb)

    forward, backward = eye, eye
    for n in range(chunks):
        xf_ref[n] = forward
        xb_ref[chunks - 1 - n] = backward
        forward = advance(forward, maps[n])
        backward = advance(backward, maps[chunks - 1 - n])
    forward = forward - eye
    backward = backward - eye
    for s in range(msg_ref.shape[0]):
        msg_ref[s] = jnp.where(s > me, forward, backward).astype(msg_ref.dtype)


def attend(text_valid, me, received, segments, link):
    groups, rows, _ = received.shape
    seglen = groups * (rows - 24)
    chunks = seglen // GROUP
    smem = pl.BlockSpec(memory_space=pltpu.SMEM)
    vmem = pl.BlockSpec(memory_space=pltpu.VMEM)
    tall = (seglen, LANES)
    return pl.pallas_call(
        attend_body,
        in_specs=[smem, smem, vmem],
        out_specs=[vmem] * 8,
        out_shape=[
            jax.ShapeDtypeStruct((segments, HDIM, LANES), link),
            jax.ShapeDtypeStruct((chunks, HDIM, LANES), f32),
            jax.ShapeDtypeStruct((chunks, HDIM, LANES), f32),
            jax.ShapeDtypeStruct(tall, bf16),
            jax.ShapeDtypeStruct(tall, bf16),
            jax.ShapeDtypeStruct(tall, bf16),
            jax.ShapeDtypeStruct(tall, bf16),
            jax.ShapeDtypeStruct(tall, f32),
        ],
        scratch_shapes=[pltpu.VMEM(tall, f32), pltpu.VMEM(tall, f32), pltpu.VMEM(tall, f32)],
        compiler_params=pltpu.CompilerParams(vmem_limit_bytes=VMEM_LIMIT),
        name="attend",
    )(text_valid, me, received)


def operators_body(xf_ref, xb_ref, kq_ref, yhi_ref, ylo_ref, att_ref, sq_ref, base_ref, ehi_ref, elo_ref):
    chunks = xf_ref.shape[0]
    row_id = lax.broadcasted_iota(jnp.int32, (GROUP, GROUP), 0)
    col_id = lax.broadcasted_iota(jnp.int32, (GROUP, GROUP), 1)
    left = lanes_left(GROUP)
    for n in range(chunks):
        at = slice(GROUP * n, GROUP * (n + 1))
        kq = kq_ref[at]
        q_first = swap_halves(kq.astype(f32))
        q = q_first[:, 0:HDIM]
        scores = mm_nt(q.astype(bf16), kq[:, 0:HDIM])
        both = jnp.concatenate(
            [jnp.where(col_id <= row_id, scores, 0.0), jnp.where(col_id >= row_id, scores, 0.0)], axis=0
        )
        both_hi, both_lo = split(both)
        y_hi, y_lo = yhi_ref[at], ylo_ref[at]
        pushed = mm(
            jnp.concatenate([both_hi, both_lo, both_hi], axis=1), jnp.concatenate([y_hi, y_hi, y_lo], axis=0)
        )
        scale = sq_ref[at]
        low, high = pushed[0:GROUP], pushed[GROUP : 2 * GROUP]
        op_f = (scale * (q_first - low))[:, 0:HDIM]
        op_b = (scale * (q_first - high))[:, 0:HDIM]
        from_f = mm3(op_f, xf_ref[n])
        from_b = mm3(op_b, xb_ref[n])
        base_ref[at] = att_ref[at].astype(f32) + scale * (low + high) + from_f + from_b
        reach = jnp.where(left, from_f, swap_halves(from_b))
        e_hi, e_lo = split(reach)
        ehi_ref[at] = e_hi
        elo_ref[at] = e_lo


def operators(xf, xb, kq, yhi, ylo, att, sq):
    tall = kq.shape
    return pl.pallas_call(
        operators_body,
        out_shape=[
            jax.ShapeDtypeStruct(tall, f32),
            jax.ShapeDtypeStruct(tall, bf16),
            jax.ShapeDtypeStruct(tall, bf16),
        ],
        compiler_params=pltpu.CompilerParams(vmem_limit_bytes=VMEM_LIMIT),
        cost_estimate=pl.CostEstimate(flops=2_000_000_000, bytes_accessed=8_000_000, transcendentals=0),
        name="operators",
    )(xf, xb, kq, yhi, ylo, att, sq)


def finish_body(me_ref, msg_ref, sf_ref, sb_ref, base_ref, ehi_ref, elo_ref, out_ref, scr):
    segments = msg_ref.shape[0]
    groups, half, _ = out_ref.shape
    me = me_ref[0]

    def follow(i, state):
        m = msg_ref[i].astype(f32)
        return state + mm3(m[:, 0:HDIM], state) + m[:, HDIM:LANES]

    w_f = lax.fori_loop(0, me, follow, sf_ref[0])
    w_b = lax.fori_loop(0, segments - 1 - me, lambda j, state: follow(segments - 1 - j, state), sb_ref[0])
    w = jnp.concatenate([w_f, w_b], axis=0)
    w_hi, w_lo = split(jnp.concatenate([w, w], axis=1))
    e_hi = ehi_ref[...]
    got = mm(jnp.concatenate([e_hi, elo_ref[...]], axis=1), jnp.concatenate([w_hi, w_hi], axis=0)) + mm(e_hi, w_lo)
    scr[...] = got + base_ref[...]
    left = lanes_left(half)
    for g in range(groups):
        first = scr[2 * half * g : 2 * half * g + half]
        second = scr[2 * half * g + half : 2 * half * (g + 1)]
        out_ref[g] = jnp.where(left, swap_halves(first), second).astype(bf16)


def finish(me, maps, state_fwd, state_bwd, base, ehi, elo, groups):
    seglen = base.shape[0]
    half = seglen // groups // 2
    smem = pl.BlockSpec(memory_space=pltpu.SMEM)
    vmem = pl.BlockSpec(memory_space=pltpu.VMEM)
    return pl.pallas_call(
        finish_body,
        in_specs=[smem] + [vmem] * 6,
        out_specs=vmem,
        out_shape=jax.ShapeDtypeStruct((groups, half, LANES), bf16),
        scratch_shapes=[pltpu.VMEM((seglen, LANES), f32)],
        compiler_params=pltpu.CompilerParams(vmem_limit_bytes=VMEM_LIMIT),
        name="finish",
    )(me, maps, state_fwd, state_bwd, base, ehi, elo)


def unpack_body(x_ref, out_ref, scr):
    heads, half, _ = x_ref.shape
    left = lanes_left(half)
    for p in range(heads // 2):
        even = x_ref[2 * p].astype(f32)
        odd = x_ref[2 * p + 1].astype(f32)
        scr[0:half] = jnp.where(left, even, swap_halves(odd))
        scr[half : 2 * half] = jnp.where(left, swap_halves(even), odd)
        out_ref[:, LANES * p : LANES * (p + 1)] = scr[...].astype(bf16)


def unpack(x):
    heads, half, _ = x.shape
    return pl.pallas_call(
        unpack_body,
        out_shape=jax.ShapeDtypeStruct((2 * half, heads * HDIM), bf16),
        scratch_shapes=[pltpu.VMEM((2 * half, LANES), f32)],
        compiler_params=pltpu.CompilerParams(vmem_limit_bytes=VMEM_LIMIT),
        name="unpack",
    )(x)


def exchange(x, axis):
    return lax.all_to_all(x, axis, split_axis=0, concat_axis=0, tiled=True)


def local(queries, keys, values, rates, text_valid, state_fwd, state_bwd):
    segments = lax.axis_size("seg")
    groups = lax.axis_size("grp")
    me = lax.axis_index("seg").astype(jnp.int32).reshape(1)
    received = exchange(pack(queries, keys, values, rates.T), "grp")
    msg, xf, xb, kq, yhi, ylo, att, sq = attend(text_valid, me, received, segments, f32)
    maps = exchange(msg, "seg")
    base, ehi, elo = operators(xf, xb, kq, yhi, ylo, att, sq)
    mixed = finish(me, maps, state_fwd, state_bwd, base, ehi, elo, groups)
    return unpack(exchange(mixed, "grp"))


def solution(mesh):
    in_specs = (
        P(("seg", "grp"), None),
        P(("seg", "grp"), None),
        P(("seg", "grp"), None),
        P(("seg", "grp"), None),
        P("seg"),
        P("grp", None, None),
        P("grp", None, None),
    )
    out_specs = P(("seg", "grp"), None)
    return jax.shard_map(local, mesh=mesh, in_specs=in_specs, out_specs=out_specs, check_vma=False)
```

```python
import math

import jax
import jax.numpy as jnp
from jax import lax
from jax.experimental import pallas as pl
from jax.experimental.pallas import tpu as pltpu
from jax.sharding import PartitionSpec as P

GROUP = 64
TEXT = 128
HDIM = 64
LANES = 128
QROWS = 256
VMEM_LIMIT = 24 * 1024 * 1024
PACK_LIMIT = 62 * 1024 * 1024

bf16 = jnp.bfloat16
f32 = jnp.float32


def split(x):
    hi = x.astype(bf16)
    return hi, (x - hi.astype(f32)).astype(bf16)


def mm(a, b):
    return lax.dot_general(a, b, (((1,), (0,)), ((), ())), preferred_element_type=f32)


def mm_nt(a, b):
    return lax.dot_general(a, b, (((1,), (1,)), ((), ())), preferred_element_type=f32)


def mm_tn(a, b):
    return lax.dot_general(a, b, (((0,), (0,)), ((), ())), preferred_element_type=f32)


def lanes_left(rows):
    return lax.broadcasted_iota(jnp.int32, (rows, LANES), 1) < HDIM


def swap_halves(x):
    return pltpu.roll(x, HDIM, 1)


def pack_body(q_hbm, k_hbm, v_hbm, r_hbm, o_ref, q_ref, k_ref, v_ref, r_ref, rate_scr, sems):
    copies = [
        pltpu.make_async_copy(source, target, sems.at[i])
        for i, (source, target) in enumerate(((r_hbm, r_ref), (q_hbm, q_ref), (k_hbm, k_ref), (v_hbm, v_ref)))
    ]
    for copy in copies:
        copy.start()
    rows, width = q_ref.shape
    heads = width // HDIM
    late = rows - 24
    left = lanes_left(rows)
    left24 = lanes_left(24)
    rate_scr[...] = jnp.zeros_like(rate_scr)
    for copy in copies:
        copy.wait()
    rate_scr[:, 0:rows] = r_ref[...].astype(f32)
    for p in range(heads // 2):
        cols = slice(LANES * p, LANES * (p + 1))
        q = q_ref[:, cols].astype(f32)
        k = k_ref[:, cols].astype(f32)
        v = v_ref[:, cols].astype(f32)
        q_sw, k_sw, v_sw = swap_halves(q), swap_halves(k), swap_halves(v)
        for odd in (0, 1):
            head = 2 * p + odd
            qk = jnp.where(left, q_sw, k) if odd else jnp.where(left, q, k_sw)
            v_right, v_left = (v, v_sw) if odd else (v_sw, v)
            rate = jnp.broadcast_to(rate_scr[head : head + 1, :], (24 - late, LANES))
            low = jnp.concatenate([v_left[24:rows], rate], axis=0)
            vr = jnp.where(left24, low, v_right[0:24])
            o_ref[head] = jnp.concatenate([qk, vr], axis=0).astype(bf16)


def pack(queries, keys, values, rates_t):
    rows, width = queries.shape
    heads = width // HDIM
    return pl.pallas_call(
        pack_body,
        in_specs=[pl.BlockSpec(memory_space=pl.ANY)] * 4,
        out_shape=jax.ShapeDtypeStruct((heads, rows + 24, LANES), bf16),
        scratch_shapes=[
            pltpu.VMEM((rows, width), bf16),
            pltpu.VMEM((rows, width), bf16),
            pltpu.VMEM((rows, width), bf16),
            pltpu.VMEM((heads, rows), bf16),
            pltpu.VMEM((heads, LANES), f32),
            pltpu.SemaphoreType.DMA((4,)),
        ],
        compiler_params=pltpu.CompilerParams(vmem_limit_bytes=PACK_LIMIT),
        name="pack",
    )(queries, keys, values, rates_t)


def packed(x):
    hi, lo = split(x)
    return jnp.where(lanes_left(x.shape[0]), hi.astype(f32), lo.astype(f32)).astype(bf16)


def twice(p):
    return jnp.concatenate([p, p], axis=1)


def four(hi, lo):
    return jnp.concatenate([hi, hi, lo, lo], axis=0)


def doubled_eye():
    row = lax.broadcasted_iota(jnp.int32, (HDIM, LANES), 0)
    col = lax.broadcasted_iota(jnp.int32, (HDIM, LANES), 1)
    return jnp.where(row == lax.rem(col, HDIM), 1.0, 0.0).astype(f32)


def attend_body(
    tv_ref, me_ref, recv_ref, msg_ref, q2_ref, k2_ref, ckh_ref, ckl_ref, dah_ref, dal_ref, att_ref, sq_ref, g_ref,
    qk_scr, v_scr, r_scr, qs_scr, step_scr, kf_scr, kb_scr,
):
    groups, rows, _ = recv_ref.shape
    toks = rows - 24
    late = toks - 24
    seglen = groups * toks
    chunks = seglen // GROUP
    blocks = seglen // QROWS
    valid = tv_ref[0]
    me = me_ref[0]

    pick = lax.broadcasted_iota(jnp.int32, (toks, LANES), 0) == lax.broadcasted_iota(jnp.int32, (toks, LANES), 1)
    left24, left_late = lanes_left(24), lanes_left(late)
    for g in range(groups):
        block = recv_ref[g].astype(f32)
        base = toks * g
        qk_scr[base : base + toks] = block[0:toks]
        tail = block[toks : toks + 24]
        tail_sw = swap_halves(tail)
        v_scr[base : base + 24] = jnp.where(left24, tail_sw, tail)
        v_scr[base + 24 : base + toks] = jnp.where(left_late, tail[0:late], tail_sw[0:late])
        r_scr[base : base + toks] = jnp.where(pick, tail[late : late + 1], 0.0)

    row_id = lax.broadcasted_iota(jnp.int32, (2 * LANES, 2 * LANES), 0)
    col_id = lax.broadcasted_iota(jnp.int32, (2 * LANES, 2 * LANES), 1)
    is_key_row = lax.rem(row_id, LANES) >= HDIM
    sums = jnp.where(is_key_row == (col_id < LANES), 1.0, 0.0).astype(bf16)
    ones = jnp.ones((LANES, LANES), bf16)
    left = lanes_left(QROWS)
    cols = lax.broadcasted_iota(jnp.int32, (QROWS, TEXT), 1)

    for b in range(blocks):
        at = slice(QROWS * b, QROWS * (b + 1))
        qk = qk_scr[at]
        kq = swap_halves(qk)
        k2 = jnp.where(left, kq, qk)
        k2_ref[at] = k2.astype(bf16)
        q2_ref[at] = jnp.where(left, qk, kq).astype(bf16)
        qs_scr[at] = jnp.where(left, qk * (1.0 / math.sqrt(HDIM)), 0.0).astype(bf16)
        squares_hi, squares_lo = split(qk * qk)
        inv = lax.rsqrt(mm(jnp.concatenate([squares_hi, squares_lo], axis=1), sums) + 1e-06)
        inv_k = inv[:, 0:LANES]
        sq_ref[at] = math.sqrt(HDIM) * inv[:, LANES : 2 * LANES]
        rate = mm(r_scr[at].astype(bf16), ones)
        if QROWS * b < TEXT:
            position = QROWS * b + lax.broadcasted_iota(jnp.int32, (QROWS, LANES), 0)
            rate = jnp.where((position >= TEXT) | (position < valid), rate, 0.0)
        step = rate * inv_k
        step_scr[at] = step
        ck_hi, ck_lo = split(step * inv_k * k2)
        ckh_ref[at] = ck_hi
        ckl_ref[at] = ck_lo

    for n in range(chunks):
        at = slice(GROUP * n, GROUP * (n + 1))
        k = k2_ref[at, 0:HDIM]
        gram = mm_tn(jnp.concatenate([k, k], axis=0), jnp.concatenate([ckh_ref[at], ckl_ref[at]], axis=0))
        g_hi, g_lo = split(gram)
        g_ref[n, 0:HDIM] = g_hi
        g_ref[n, HDIM : 2 * HDIM] = g_lo

    v2 = v_scr[...].astype(bf16)
    eye = doubled_eye()
    t_f, t_b = eye, eye

    def advance(t, n, keep_ref):
        at = slice(GROUP * n, GROUP * (n + 1))
        p = packed(t)
        keep_ref[at] = packed(mm_nt(k2_ref[at], jnp.concatenate([p, p], axis=0)))
        return t - mm(twice(p), four(g_ref[n, 0:HDIM], g_ref[n, HDIM : 2 * HDIM]))

    for b in range(blocks):
        at = slice(QROWS * b, QROWS * (b + 1))
        scores = mm_nt(qs_scr[at], k2_ref[...])
        for n in range(chunks * b // blocks, chunks * (b + 1) // blocks):
            t_f = advance(t_f, n, kf_scr)
            t_b = advance(t_b, chunks - 1 - n, kb_scr)
        head_part = jnp.where(cols < valid, scores[:, 0:TEXT], -1e30)
        scores = jnp.concatenate([head_part, scores[:, TEXT:]], axis=1)
        peak = jnp.max(scores, axis=1, keepdims=True)
        raised = jnp.exp(scores - peak)
        row_total = jnp.sum(raised, axis=1, keepdims=True)
        gathered = mm(raised.astype(bf16), v2)
        att = (gathered / row_total).astype(bf16)
        att_ref[at] = att
        da_hi, da_lo = split(step_scr[at] * att.astype(f32))
        dah_ref[at] = da_hi
        dal_ref[at] = da_lo

    total = jnp.zeros((LANES, 2 * LANES), f32)
    for b in range(blocks):
        at = slice(QROWS * b, QROWS * (b + 1))
        da = jnp.where(left, dah_ref[at].astype(f32), dal_ref[at].astype(f32)).astype(bf16)
        total = total + mm_tn(da, jnp.concatenate([kf_scr[at], kb_scr[at]], axis=1))
    total = total[0:HDIM] + total[HDIM : 2 * HDIM]
    from_f, from_b = total[:, 0:LANES], total[:, LANES : 2 * LANES]
    shift_b = from_f + swap_halves(from_f)
    shift_f = from_b + swap_halves(from_b)
    left64 = lanes_left(HDIM)
    later = jnp.where(left64, t_f - eye, shift_f)
    earlier = jnp.where(left64, t_b - eye, shift_b)
    for s in range(msg_ref.shape[0]):
        msg_ref[s] = jnp.where(s > me, later, earlier).astype(msg_ref.dtype)


def attend(text_valid, me, received, segments, link):
    groups, rows, _ = received.shape
    seglen = groups * (rows - 24)
    chunks = seglen // GROUP
    smem = pl.BlockSpec(memory_space=pltpu.SMEM)
    vmem = pl.BlockSpec(memory_space=pltpu.VMEM)
    tall = (seglen, LANES)
    return pl.pallas_call(
        attend_body,
        in_specs=[smem, smem, vmem],
        out_specs=[vmem] * 10,
        out_shape=[jax.ShapeDtypeStruct((segments, HDIM, LANES), link)]
        + [jax.ShapeDtypeStruct(tall, bf16)] * 7
        + [jax.ShapeDtypeStruct(tall, f32), jax.ShapeDtypeStruct((chunks, LANES, LANES), bf16)],
        scratch_shapes=[
            pltpu.VMEM(tall, f32), pltpu.VMEM(tall, f32), pltpu.VMEM(tall, f32), pltpu.VMEM(tall, bf16),
            pltpu.VMEM(tall, f32), pltpu.VMEM(tall, bf16), pltpu.VMEM(tall, bf16),
        ],
        compiler_params=pltpu.CompilerParams(vmem_limit_bytes=VMEM_LIMIT),
        name="attend",
    )(text_valid, me, received)


def operators_body(
    q2_ref, k2_ref, ckh_ref, ckl_ref, dah_ref, dal_ref, att_ref, sq_ref, g_ref, base_ref, ehi_ref, elo_ref,
    opf_scr, opb_scr, xf_scr, xb_scr,
):
    chunks = g_ref.shape[0]
    row_id = lax.broadcasted_iota(jnp.int32, (GROUP, LANES), 0)
    col_id = lax.rem(lax.broadcasted_iota(jnp.int32, (GROUP, LANES), 1), GROUP)
    left = lanes_left(GROUP)
    eye = doubled_eye()
    x_f = jnp.concatenate([eye, jnp.zeros_like(eye)], axis=0)
    x_b = x_f

    def rows_of(n):
        return slice(GROUP * n, GROUP * (n + 1))

    def advance(x, n, keep_ref):
        at = rows_of(n)
        hi, lo = split(x)
        keep_ref[n] = jnp.concatenate([hi, lo], axis=1)
        p = jnp.where(lanes_left(2 * HDIM), hi.astype(f32), lo.astype(f32)).astype(bf16)
        k2 = k2_ref[at]
        pushed = mm_tn(
            jnp.concatenate([dah_ref[at, 0:HDIM], dal_ref[at, 0:HDIM]], axis=0), jnp.concatenate([k2, k2], axis=0)
        )
        x = x - mm(twice(p), four(g_ref[n, 0:HDIM], g_ref[n, HDIM : 2 * HDIM]))
        return jnp.concatenate([x[0:HDIM], x[HDIM : 2 * HDIM] + pushed], axis=0)

    for n in range(chunks):
        x_f = advance(x_f, n, xf_scr)
        x_b = advance(x_b, chunks - 1 - n, xb_scr)
        at = rows_of(n)
        k2, q2 = k2_ref[at], q2_ref[at]
        scores = mm_nt(q2[:, 0:HDIM], jnp.concatenate([k2, k2], axis=0)[:, 0:HDIM])
        both = packed(
            jnp.concatenate(
                [jnp.where(col_id <= row_id, scores, 0.0), jnp.where(col_id >= row_id, scores, 0.0)], axis=0
            )
        )
        y_hi = jnp.concatenate([ckh_ref[at], dah_ref[at]], axis=1)
        y_lo = jnp.concatenate([ckl_ref[at], dal_ref[at]], axis=1)
        pushed = mm(twice(both), four(y_hi, y_lo))
        scale = sq_ref[at]
        q = q2.astype(f32)
        opf_scr[at] = packed(scale * (q - pushed[0:GROUP, 0:LANES]))
        opb_scr[at] = packed(scale * (q - pushed[GROUP : 2 * GROUP, 0:LANES]))
        base_ref[at] = att_ref[at].astype(f32) + scale * (
            pushed[0:GROUP, LANES : 2 * LANES] + pushed[GROUP : 2 * GROUP, LANES : 2 * LANES]
        )

    for n in range(chunks):
        at = rows_of(n)

        def through(op_ref, x_ref):
            t, w = x_ref[n, 0:HDIM], x_ref[n, HDIM : 2 * HDIM]
            return mm_nt(twice(op_ref[at]), jnp.concatenate([t, t, w, w], axis=0))

        from_f, from_b = through(opf_scr, xf_scr), through(opb_scr, xb_scr)
        base_ref[at] = base_ref[at] + from_f[:, LANES : 2 * LANES] + from_b[:, LANES : 2 * LANES]
        e_hi, e_lo = split(jnp.where(left, from_f[:, 0:LANES], from_b[:, 0:LANES]))
        ehi_ref[at] = e_hi
        elo_ref[at] = e_lo


def operators(*held):
    tall = held[0].shape
    chunks = tall[0] // GROUP
    state = (chunks, 2 * HDIM, 2 * LANES)
    return pl.pallas_call(
        operators_body,
        out_shape=[
            jax.ShapeDtypeStruct(tall, f32),
            jax.ShapeDtypeStruct(tall, bf16),
            jax.ShapeDtypeStruct(tall, bf16),
        ],
        scratch_shapes=[
            pltpu.VMEM(tall, bf16), pltpu.VMEM(tall, bf16), pltpu.VMEM(state, bf16), pltpu.VMEM(state, bf16),
        ],
        compiler_params=pltpu.CompilerParams(vmem_limit_bytes=VMEM_LIMIT),
        cost_estimate=pl.CostEstimate(flops=2_000_000_000, bytes_accessed=8_000_000, transcendentals=0),
        name="operators",
    )(*held)


def finish_body(me_ref, msg_ref, sf_ref, sb_ref, base_ref, ehi_ref, elo_ref, out_ref, scr):
    segments = msg_ref.shape[0]
    groups, half, _ = out_ref.shape
    me = me_ref[0]
    left64 = lanes_left(HDIM)

    def doubled_transpose(state):
        return jnp.concatenate([state, state], axis=0).T

    def follow(i, live, state):
        m = jnp.where(live, msg_ref[i].astype(f32), 0.0)
        m_sw = swap_halves(m)
        decay = jnp.where(left64, m, m_sw)
        shift = jnp.where(left64, m_sw, m)
        hi, lo = split(decay)
        return state + mm(twice(packed(state)), four(hi, lo)) + shift

    w_f, w_b = doubled_transpose(sf_ref[0]), doubled_transpose(sb_ref[0])
    for i in range(segments - 1):
        w_f = follow(i, i < me, w_f)
        w_b = follow(segments - 1 - i, segments - 1 - i > me, w_b)
    w_hi, w_lo = split(jnp.where(left64, w_f, w_b))
    w_row = jnp.concatenate([w_hi, w_hi, w_lo], axis=1)
    e_hi = ehi_ref[...]
    got = mm_nt(jnp.concatenate([e_hi, elo_ref[...], e_hi], axis=1), jnp.concatenate([w_row, w_row], axis=0))
    scr[...] = got + base_ref[...]
    left = lanes_left(half)
    for g in range(groups):
        first = scr[2 * half * g : 2 * half * g + half]
        second = scr[2 * half * g + half : 2 * half * (g + 1)]
        out_ref[g] = jnp.where(left, first, second).astype(bf16)


def finish(me, maps, state_fwd, state_bwd, base, ehi, elo, groups):
    seglen = base.shape[0]
    half = seglen // groups // 2
    smem = pl.BlockSpec(memory_space=pltpu.SMEM)
    vmem = pl.BlockSpec(memory_space=pltpu.VMEM)
    return pl.pallas_call(
        finish_body,
        in_specs=[smem] + [vmem] * 6,
        out_specs=vmem,
        out_shape=jax.ShapeDtypeStruct((groups, half, LANES), bf16),
        scratch_shapes=[pltpu.VMEM((seglen, LANES), f32)],
        compiler_params=pltpu.CompilerParams(vmem_limit_bytes=VMEM_LIMIT),
        name="finish",
    )(me, maps, state_fwd, state_bwd, base, ehi, elo)


def unpack_body(x_ref, out_ref, scr):
    heads, half, _ = x_ref.shape
    left = lanes_left(half)
    for p in range(heads // 2):
        even = x_ref[2 * p].astype(f32)
        odd = x_ref[2 * p + 1].astype(f32)
        scr[0:half] = jnp.where(left, even, swap_halves(odd))
        scr[half : 2 * half] = jnp.where(left, swap_halves(even), odd)
        out_ref[:, LANES * p : LANES * (p + 1)] = scr[...].astype(bf16)


def unpack(x):
    heads, half, _ = x.shape
    return pl.pallas_call(
        unpack_body,
        out_shape=jax.ShapeDtypeStruct((2 * half, heads * HDIM), bf16),
        scratch_shapes=[pltpu.VMEM((2 * half, LANES), f32)],
        compiler_params=pltpu.CompilerParams(vmem_limit_bytes=VMEM_LIMIT),
        name="unpack",
    )(x)


def exchange(x, axis):
    return lax.all_to_all(x, axis, split_axis=0, concat_axis=0, tiled=True)


def local(queries, keys, values, rates, text_valid, state_fwd, state_bwd):
    segments = lax.axis_size("seg")
    groups = lax.axis_size("grp")
    me = lax.axis_index("seg").astype(jnp.int32).reshape(1)
    received = exchange(pack(queries, keys, values, rates.T), "grp")
    msg, *held = attend(text_valid, me, received, segments, bf16)
    maps = exchange(msg, "seg")
    base, ehi, elo = operators(*held)
    mixed = finish(me, maps, state_fwd, state_bwd, base, ehi, elo, groups)
    return unpack(exchange(mixed, "grp"))


def solution(mesh):
    in_specs = (
        P(("seg", "grp"), None),
        P(("seg", "grp"), None),
        P(("seg", "grp"), None),
        P(("seg", "grp"), None),
        P("seg"),
        P("grp", None, None),
        P("grp", None, None),
    )
    out_specs = P(("seg", "grp"), None)
    return jax.shard_map(local, mesh=mesh, in_specs=in_specs, out_specs=out_specs, check_vma=False)
```

```python
import math

import jax
import jax.numpy as jnp
from jax import lax
from jax.experimental import pallas as pl
from jax.experimental.pallas import tpu as pltpu
from jax.sharding import PartitionSpec as P

GROUP = 64
TEXT = 128
HDIM = 64
LANES = 128
QROWS = 256
AROWS = 128
VMEM_LIMIT = 24 * 1024 * 1024
PACK_LIMIT = 62 * 1024 * 1024

bf16 = jnp.bfloat16
f32 = jnp.float32


def split(x):
    hi = x.astype(bf16)
    return hi, (x - hi.astype(f32)).astype(bf16)


def mm(a, b):
    return lax.dot_general(a, b, (((1,), (0,)), ((), ())), preferred_element_type=f32)


def mm_nt(a, b):
    return lax.dot_general(a, b, (((1,), (1,)), ((), ())), preferred_element_type=f32)


def mm_tn(a, b):
    return lax.dot_general(a, b, (((0,), (0,)), ((), ())), preferred_element_type=f32)


def lanes_left(rows):
    return lax.broadcasted_iota(jnp.int32, (rows, LANES), 1) < HDIM


def swap_halves(x):
    return pltpu.roll(x, HDIM, 1)


def pack_body(q_hbm, k_hbm, v_hbm, r_hbm, o_ref, q_ref, k_ref, v_ref, r_ref, rate_scr, sems):
    copies = [
        pltpu.make_async_copy(source, target, sems.at[i])
        for i, (source, target) in enumerate(((r_hbm, r_ref), (q_hbm, q_ref), (k_hbm, k_ref), (v_hbm, v_ref)))
    ]
    for copy in copies:
        copy.start()
    rows, width = q_ref.shape
    heads = width // HDIM
    late = rows - 24
    left = lanes_left(rows)
    left24 = lanes_left(24)
    rate_scr[...] = jnp.zeros_like(rate_scr)
    for copy in copies:
        copy.wait()
    rate_scr[:, 0:rows] = r_ref[...].astype(f32)
    for p in range(heads // 2):
        cols = slice(LANES * p, LANES * (p + 1))
        q = q_ref[:, cols].astype(f32)
        k = k_ref[:, cols].astype(f32)
        v = v_ref[:, cols].astype(f32)
        q_sw, k_sw, v_sw = swap_halves(q), swap_halves(k), swap_halves(v)
        for odd in (0, 1):
            head = 2 * p + odd
            qk = jnp.where(left, q_sw, k) if odd else jnp.where(left, q, k_sw)
            v_right, v_left = (v, v_sw) if odd else (v_sw, v)
            rate = jnp.broadcast_to(rate_scr[head : head + 1, :], (24 - late, LANES))
            low = jnp.concatenate([v_left[24:rows], rate], axis=0)
            vr = jnp.where(left24, low, v_right[0:24])
            o_ref[head] = jnp.concatenate([qk, vr], axis=0).astype(bf16)


def pack(queries, keys, values, rates_t):
    rows, width = queries.shape
    heads = width // HDIM
    return pl.pallas_call(
        pack_body,
        in_specs=[pl.BlockSpec(memory_space=pl.ANY)] * 4,
        out_shape=jax.ShapeDtypeStruct((heads, rows + 24, LANES), bf16),
        scratch_shapes=[
            pltpu.VMEM((rows, width), bf16),
            pltpu.VMEM((rows, width), bf16),
            pltpu.VMEM((rows, width), bf16),
            pltpu.VMEM((heads, rows), bf16),
            pltpu.VMEM((heads, LANES), f32),
            pltpu.SemaphoreType.DMA((4,)),
        ],
        compiler_params=pltpu.CompilerParams(vmem_limit_bytes=PACK_LIMIT),
        name="pack",
    )(queries, keys, values, rates_t)


def packed(x):
    hi, lo = split(x)
    return jnp.where(lanes_left(x.shape[0]), hi.astype(f32), lo.astype(f32)).astype(bf16)


def twice(p):
    return jnp.concatenate([p, p], axis=1)


def four(hi, lo):
    return jnp.concatenate([hi, hi, lo, lo], axis=0)


def doubled_eye():
    row = lax.broadcasted_iota(jnp.int32, (HDIM, LANES), 0)
    col = lax.broadcasted_iota(jnp.int32, (HDIM, LANES), 1)
    return jnp.where(row == lax.rem(col, HDIM), 1.0, 0.0).astype(f32)


def norm_sums():
    row = lax.broadcasted_iota(jnp.int32, (2 * LANES, 2 * LANES), 0)
    col = lax.broadcasted_iota(jnp.int32, (2 * LANES, 2 * LANES), 1)
    is_key_row = lax.rem(row, LANES) >= HDIM
    return jnp.where(is_key_row == (col < LANES), 1.0, 0.0).astype(bf16)


def inverse_norms(qk, sums):
    hi, lo = split(qk * qk)
    return lax.rsqrt(mm(jnp.concatenate([hi, lo], axis=1), sums) + 1e-06)


def attend_body(
    tv_ref, me_ref, recv_ref, msg_ref, qk_ref, ar_ref, g_ref,
    qk_scr, v_scr, r_scr, inv_scr, rate_scr, k2_scr, qs_scr, kf_scr, kb_scr, da_scr, ckh_scr, ckl_scr,
):
    groups, rows, _ = recv_ref.shape
    toks = rows - 24
    late = toks - 24
    seglen = groups * toks
    chunks = seglen // GROUP
    blocks = seglen // QROWS
    valid = tv_ref[0]
    me = me_ref[0]

    pick = lax.broadcasted_iota(jnp.int32, (toks, LANES), 0) == lax.broadcasted_iota(jnp.int32, (toks, LANES), 1)
    left24, left_late = lanes_left(24), lanes_left(late)
    for g in range(groups):
        block = recv_ref[g].astype(f32)
        base = toks * g
        qk_scr[base : base + toks] = block[0:toks]
        tail = block[toks : toks + 24]
        tail_sw = swap_halves(tail)
        v_scr[base : base + 24] = jnp.where(left24, tail_sw, tail)
        v_scr[base + 24 : base + toks] = jnp.where(left_late, tail[0:late], tail_sw[0:late])
        r_scr[base : base + toks] = jnp.where(pick, tail[late : late + 1], 0.0)

    sums = norm_sums()
    ones = jnp.ones((LANES, LANES), bf16)
    left = lanes_left(QROWS)

    for b in range(blocks):
        at = slice(QROWS * b, QROWS * (b + 1))
        inv_scr[at] = inverse_norms(qk_scr[at], sums)[:, 0:LANES]
        rate = mm(r_scr[at].astype(bf16), ones)
        if QROWS * b < TEXT:
            position = QROWS * b + lax.broadcasted_iota(jnp.int32, (QROWS, LANES), 0)
            rate = jnp.where((position >= TEXT) | (position < valid), rate, 0.0)
        rate_scr[at] = rate
    for b in range(blocks):
        at = slice(QROWS * b, QROWS * (b + 1))
        qk = qk_scr[at]
        kq = swap_halves(qk)
        k2 = jnp.where(left, kq, qk)
        k2_scr[at] = k2.astype(bf16)
        qk_ref[at] = qk.astype(bf16)
        qs_scr[at] = jnp.where(left, qk * (1.0 / math.sqrt(HDIM)), 0.0).astype(bf16)
        inv_k = inv_scr[at]
        step = rate_scr[at] * inv_k
        inv_scr[at] = step
        ck_hi, ck_lo = split(step * inv_k * k2)
        ckh_scr[at] = ck_hi
        ckl_scr[at] = ck_lo
    for n in range(chunks):
        at = slice(GROUP * n, GROUP * (n + 1))
        k = k2_scr[at, 0:HDIM]
        gram = mm_tn(jnp.concatenate([k, k], axis=0), jnp.concatenate([ckh_scr[at], ckl_scr[at]], axis=0))
        g_hi, g_lo = split(gram)
        g_ref[n, 0:HDIM] = g_hi
        g_ref[n, HDIM : 2 * HDIM] = g_lo

    v2 = v_scr[...].astype(bf16)
    eye = doubled_eye()
    t_f, t_b = eye, eye

    def advance(t, n, keep_ref):
        at = slice(GROUP * n, GROUP * (n + 1))
        p = packed(t)
        keep_ref[at] = packed(mm_nt(k2_scr[at], jnp.concatenate([p, p], axis=0)))
        return t - mm(twice(p), four(g_ref[n, 0:HDIM], g_ref[n, HDIM : 2 * HDIM]))

    parts = seglen // AROWS
    cols = lax.broadcasted_iota(jnp.int32, (AROWS, TEXT), 1)
    left_part = lanes_left(AROWS)

    def scores_of(b):
        scores = mm_nt(qs_scr[AROWS * b : AROWS * (b + 1)], k2_scr[...])
        return jnp.concatenate([jnp.where(cols < valid, scores[:, 0:TEXT], -1e30), scores[:, TEXT:]], axis=1)

    scores = scores_of(0)
    for b in range(parts):
        at = slice(AROWS * b, AROWS * (b + 1))
        following = scores_of(b + 1) if b + 1 < parts else None
        for n in range(chunks * b // parts, chunks * (b + 1) // parts):
            t_f = advance(t_f, n, kf_scr)
            t_b = advance(t_b, chunks - 1 - n, kb_scr)
        peak = jnp.max(scores, axis=1, keepdims=True)
        raised = jnp.exp(scores - peak)
        row_total = jnp.sum(raised, axis=1, keepdims=True)
        att = (mm(raised.astype(bf16), v2) / row_total).astype(bf16).astype(f32)
        ar_ref[at] = jnp.where(left_part, att, rate_scr[at]).astype(bf16)
        da_scr[at] = packed(inv_scr[at] * att)
        scores = following

    total = jnp.zeros((LANES, 2 * LANES), f32)
    for b in range(blocks):
        at = slice(QROWS * b, QROWS * (b + 1))
        total = total + mm_tn(da_scr[at], jnp.concatenate([kf_scr[at], kb_scr[at]], axis=1))
    total = total[0:HDIM] + total[HDIM : 2 * HDIM]
    from_f, from_b = total[:, 0:LANES], total[:, LANES : 2 * LANES]
    shift_b = from_f + swap_halves(from_f)
    shift_f = from_b + swap_halves(from_b)
    left64 = lanes_left(HDIM)
    later = jnp.where(left64, t_f - eye, shift_f)
    earlier = jnp.where(left64, t_b - eye, shift_b)
    for s in range(msg_ref.shape[0]):
        msg_ref[s] = jnp.where(s > me, later, earlier).astype(msg_ref.dtype)


def attend(text_valid, me, received, segments, link):
    groups, rows, _ = received.shape
    seglen = groups * (rows - 24)
    chunks = seglen // GROUP
    smem = pl.BlockSpec(memory_space=pltpu.SMEM)
    vmem = pl.BlockSpec(memory_space=pltpu.VMEM)
    tall = (seglen, LANES)
    return pl.pallas_call(
        attend_body,
        in_specs=[smem, smem, vmem],
        out_specs=[vmem] * 4,
        out_shape=[jax.ShapeDtypeStruct((segments, HDIM, LANES), link)]
        + [jax.ShapeDtypeStruct(tall, bf16)] * 2
        + [jax.ShapeDtypeStruct((chunks, LANES, LANES), bf16)],
        scratch_shapes=[
            *[pltpu.VMEM(tall, f32)] * 5, *[pltpu.VMEM(tall, bf16)] * 7,
        ],
        compiler_params=pltpu.CompilerParams(vmem_limit_bytes=VMEM_LIMIT),
        name="attend",
    )(text_valid, me, received)


def operators_body(
    qk_ref, ar_ref, g_ref, base_ref, ehi_ref, elo_ref,
    opf_scr, opb_scr, xf_scr, xb_scr, shift_scr, yhi_scr, ylo_scr, k2_scr, q2_scr, inv_scr,
):
    chunks = g_ref.shape[0]
    row_id = lax.broadcasted_iota(jnp.int32, (GROUP, LANES), 0)
    col_id = lax.rem(lax.broadcasted_iota(jnp.int32, (GROUP, LANES), 1), GROUP)
    left = lanes_left(GROUP)
    sums = norm_sums()
    eye = doubled_eye()
    x_f = jnp.concatenate([eye, jnp.zeros_like(eye)], axis=0)
    x_b = x_f

    def rows_of(n):
        return slice(GROUP * n, GROUP * (n + 1))

    def halves(x):
        x = x.astype(f32)
        x_sw = swap_halves(x)
        on_left = lanes_left(x.shape[0])
        return jnp.where(on_left, x, x_sw), jnp.where(on_left, x_sw, x)

    def advance(x, n, keep_ref):
        hi, lo = split(x)
        keep_ref[n] = jnp.concatenate([hi, lo], axis=1)
        p = jnp.where(lanes_left(2 * HDIM), hi.astype(f32), lo.astype(f32)).astype(bf16)
        x = x - mm(twice(p), four(g_ref[n, 0:HDIM], g_ref[n, HDIM : 2 * HDIM]))
        return jnp.concatenate([x[0:HDIM], x[HDIM : 2 * HDIM] + shift_scr[n]], axis=0)

    blocks = chunks * GROUP // QROWS
    for b in range(blocks):
        at = slice(QROWS * b, QROWS * (b + 1))
        inv_scr[at] = inverse_norms(qk_ref[at].astype(f32), sums)
    for b in range(blocks):
        at = slice(QROWS * b, QROWS * (b + 1))
        inv_k = inv_scr[at, 0:LANES]
        q2, k2 = halves(qk_ref[at])
        att, rate = halves(ar_ref[at])
        step = rate * inv_k
        ck_hi, ck_lo = split(step * inv_k * k2)
        da_hi, da_lo = split(step * att)
        yhi_scr[at] = jnp.concatenate([ck_hi, da_hi], axis=1)
        ylo_scr[at] = jnp.concatenate([ck_lo, da_lo], axis=1)
        base_ref[at] = att
        q2_scr[at] = q2.astype(bf16)
        k2_scr[at] = k2.astype(bf16)
    for n in range(chunks):
        at = rows_of(n)
        k2 = k2_scr[at]
        da = jnp.concatenate([yhi_scr[at, LANES : LANES + HDIM], ylo_scr[at, LANES : LANES + HDIM]], axis=0)
        shift_scr[n] = mm_tn(da, jnp.concatenate([k2, k2], axis=0))

    for n in range(chunks):
        x_f = advance(x_f, n, xf_scr)
        x_b = advance(x_b, chunks - 1 - n, xb_scr)
        at = rows_of(n)
        q2, k2 = q2_scr[at], k2_scr[at]
        scores = mm_nt(q2[:, 0:HDIM], jnp.concatenate([k2, k2], axis=0)[:, 0:HDIM])
        both = packed(
            jnp.concatenate(
                [jnp.where(col_id <= row_id, scores, 0.0), jnp.where(col_id >= row_id, scores, 0.0)], axis=0
            )
        )
        y_hi, y_lo = yhi_scr[at], ylo_scr[at]
        pushed = mm(twice(both), four(y_hi, y_lo))
        scale = math.sqrt(HDIM) * inv_scr[at, LANES : 2 * LANES]
        q = q2.astype(f32)
        opf_scr[at] = packed(scale * (q - pushed[0:GROUP, 0:LANES]))
        opb_scr[at] = packed(scale * (q - pushed[GROUP : 2 * GROUP, 0:LANES]))
        base_ref[at] = base_ref[at] + scale * (
            pushed[0:GROUP, LANES : 2 * LANES] + pushed[GROUP : 2 * GROUP, LANES : 2 * LANES]
        )

    for n in range(chunks):
        at = rows_of(n)

        def through(op_ref, x_ref):
            t, w = x_ref[n, 0:HDIM], x_ref[n, HDIM : 2 * HDIM]
            return mm_nt(twice(op_ref[at]), jnp.concatenate([t, t, w, w], axis=0))

        from_f, from_b = through(opf_scr, xf_scr), through(opb_scr, xb_scr)
        base_ref[at] = base_ref[at] + from_f[:, LANES : 2 * LANES] + from_b[:, LANES : 2 * LANES]
        e_hi, e_lo = split(jnp.where(left, from_f[:, 0:LANES], from_b[:, 0:LANES]))
        ehi_ref[at] = e_hi
        elo_ref[at] = e_lo


def operators(*held):
    tall = held[0].shape
    chunks = tall[0] // GROUP
    state = (chunks, 2 * HDIM, 2 * LANES)
    return pl.pallas_call(
        operators_body,
        out_shape=[
            jax.ShapeDtypeStruct(tall, f32),
            jax.ShapeDtypeStruct(tall, bf16),
            jax.ShapeDtypeStruct(tall, bf16),
        ],
        scratch_shapes=[
            pltpu.VMEM(tall, bf16), pltpu.VMEM(tall, bf16), pltpu.VMEM(state, bf16), pltpu.VMEM(state, bf16),
            pltpu.VMEM((chunks, HDIM, LANES), f32),
            pltpu.VMEM((tall[0], 2 * LANES), bf16), pltpu.VMEM((tall[0], 2 * LANES), bf16),
            pltpu.VMEM(tall, bf16), pltpu.VMEM(tall, bf16), pltpu.VMEM((tall[0], 2 * LANES), f32),
        ],
        compiler_params=pltpu.CompilerParams(vmem_limit_bytes=VMEM_LIMIT),
        cost_estimate=pl.CostEstimate(flops=2_000_000_000, bytes_accessed=8_000_000, transcendentals=0),
        name="operators",
    )(*held)


def finish_body(me_ref, msg_ref, sf_ref, sb_ref, base_ref, ehi_ref, elo_ref, out_ref, scr):
    segments = msg_ref.shape[0]
    groups, half, _ = out_ref.shape
    me = me_ref[0]
    left64 = lanes_left(HDIM)

    def doubled_transpose(state):
        return jnp.concatenate([state, state], axis=0).T

    def follow(i, live, state):
        m = jnp.where(live, msg_ref[i].astype(f32), 0.0)
        m_sw = swap_halves(m)
        decay = jnp.where(left64, m, m_sw)
        shift = jnp.where(left64, m_sw, m)
        hi, lo = split(decay)
        return state + mm(twice(packed(state)), four(hi, lo)) + shift

    w_f, w_b = doubled_transpose(sf_ref[0]), doubled_transpose(sb_ref[0])
    for i in range(segments - 1):
        w_f = follow(i, i < me, w_f)
        w_b = follow(segments - 1 - i, segments - 1 - i > me, w_b)
    w_hi, w_lo = split(jnp.where(left64, w_f, w_b))
    w_row = jnp.concatenate([w_hi, w_hi, w_lo], axis=1)
    e_hi = ehi_ref[...]
    got = mm_nt(jnp.concatenate([e_hi, elo_ref[...], e_hi], axis=1), jnp.concatenate([w_row, w_row], axis=0))
    scr[...] = got + base_ref[...]
    left = lanes_left(half)
    for g in range(groups):
        first = scr[2 * half * g : 2 * half * g + half]
        second = scr[2 * half * g + half : 2 * half * (g + 1)]
        out_ref[g] = jnp.where(left, first, second).astype(bf16)


def finish(me, maps, state_fwd, state_bwd, base, ehi, elo, groups):
    seglen = base.shape[0]
    half = seglen // groups // 2
    smem = pl.BlockSpec(memory_space=pltpu.SMEM)
    vmem = pl.BlockSpec(memory_space=pltpu.VMEM)
    return pl.pallas_call(
        finish_body,
        in_specs=[smem] + [vmem] * 6,
        out_specs=vmem,
        out_shape=jax.ShapeDtypeStruct((groups, half, LANES), bf16),
        scratch_shapes=[pltpu.VMEM((seglen, LANES), f32)],
        compiler_params=pltpu.CompilerParams(vmem_limit_bytes=VMEM_LIMIT),
        name="finish",
    )(me, maps, state_fwd, state_bwd, base, ehi, elo)


def unpack_body(x_ref, out_ref, scr):
    heads, half, _ = x_ref.shape
    left = lanes_left(half)
    for p in range(heads // 2):
        even = x_ref[2 * p].astype(f32)
        odd = x_ref[2 * p + 1].astype(f32)
        scr[0:half] = jnp.where(left, even, swap_halves(odd))
        scr[half : 2 * half] = jnp.where(left, swap_halves(even), odd)
        out_ref[:, LANES * p : LANES * (p + 1)] = scr[...].astype(bf16)


def unpack(x):
    heads, half, _ = x.shape
    return pl.pallas_call(
        unpack_body,
        out_shape=jax.ShapeDtypeStruct((2 * half, heads * HDIM), bf16),
        scratch_shapes=[pltpu.VMEM((2 * half, LANES), f32)],
        compiler_params=pltpu.CompilerParams(vmem_limit_bytes=VMEM_LIMIT),
        name="unpack",
    )(x)


def exchange(x, axis):
    return lax.all_to_all(x, axis, split_axis=0, concat_axis=0, tiled=True)


def local(queries, keys, values, rates, text_valid, state_fwd, state_bwd):
    segments = lax.axis_size("seg")
    groups = lax.axis_size("grp")
    me = lax.axis_index("seg").astype(jnp.int32).reshape(1)
    received = exchange(pack(queries, keys, values, rates.T), "grp")
    msg, *held = attend(text_valid, me, received, segments, bf16)
    maps = exchange(msg, "seg")
    base, ehi, elo = operators(*held)
    mixed = finish(me, maps, state_fwd, state_bwd, base, ehi, elo, groups)
    return unpack(exchange(mixed, "grp"))


def solution(mesh):
    in_specs = (
        P(("seg", "grp"), None),
        P(("seg", "grp"), None),
        P(("seg", "grp"), None),
        P(("seg", "grp"), None),
        P("seg"),
        P("grp", None, None),
        P("grp", None, None),
    )
    out_specs = P(("seg", "grp"), None)
    return jax.shard_map(local, mesh=mesh, in_specs=in_specs, out_specs=out_specs, check_vma=False)
```

```python
import math

import jax
import jax.numpy as jnp
from jax import lax
from jax.experimental import pallas as pl
from jax.experimental.pallas import tpu as pltpu
from jax.sharding import PartitionSpec as P

GROUP = 64
TEXT = 128
HDIM = 64
LANES = 128
QROWS = 256
AROWS = 128
PACK_PARTS = 2
VMEM_LIMIT = 24 * 1024 * 1024
PACK_LIMIT = 62 * 1024 * 1024

bf16 = jnp.bfloat16
f32 = jnp.float32


def split(x):
    hi = x.astype(bf16)
    return hi, (x - hi.astype(f32)).astype(bf16)


def mm(a, b):
    return lax.dot_general(a, b, (((1,), (0,)), ((), ())), preferred_element_type=f32)


def mm_nt(a, b):
    return lax.dot_general(a, b, (((1,), (1,)), ((), ())), preferred_element_type=f32)


def mm_tn(a, b):
    return lax.dot_general(a, b, (((0,), (0,)), ((), ())), preferred_element_type=f32)


def lanes_left(rows):
    return lax.broadcasted_iota(jnp.int32, (rows, LANES), 1) < HDIM


def swap_halves(x):
    return pltpu.roll(x, HDIM, 1)


def pack_body(q_hbm, k_hbm, v_hbm, r_hbm, o_hbm, q_ref, k_ref, v_ref, r_ref, o_ref, rate_scr, in_sems, out_sems):
    rows, width = q_ref.shape
    heads = width // HDIM
    late = rows - 24
    parts = in_sems.shape[0]
    wide = width // parts
    each = heads // parts
    rate_copy = pltpu.make_async_copy(r_hbm, r_ref, in_sems.at[0, 3])
    rate_copy.start()
    reads, writes = [], []
    for part in range(parts):
        cols = pl.ds(wide * part, wide)
        reads.append(
            [
                pltpu.make_async_copy(source.at[:, cols], target.at[:, cols], in_sems.at[part, i])
                for i, (source, target) in enumerate(((q_hbm, q_ref), (k_hbm, k_ref), (v_hbm, v_ref)))
            ]
        )
        for read in reads[part]:
            read.start()
    left = lanes_left(rows)
    left24 = lanes_left(24)
    rate_scr[...] = jnp.zeros_like(rate_scr)
    rate_copy.wait()
    rate_scr[:, 0:rows] = r_ref[...].astype(f32)
    for part in range(parts):
        for read in reads[part]:
            read.wait()
        for p in range(each // 2 * part, each // 2 * (part + 1)):
            cols = slice(LANES * p, LANES * (p + 1))
            q = q_ref[:, cols].astype(f32)
            k = k_ref[:, cols].astype(f32)
            v = v_ref[:, cols].astype(f32)
            q_sw, k_sw, v_sw = swap_halves(q), swap_halves(k), swap_halves(v)
            for odd in (0, 1):
                head = 2 * p + odd
                qk = jnp.where(left, q_sw, k) if odd else jnp.where(left, q, k_sw)
                v_right, v_left = (v, v_sw) if odd else (v_sw, v)
                rate = jnp.broadcast_to(rate_scr[head : head + 1, :], (24 - late, LANES))
                low = jnp.concatenate([v_left[24:rows], rate], axis=0)
                vr = jnp.where(left24, low, v_right[0:24])
                o_ref[head] = jnp.concatenate([qk, vr], axis=0).astype(bf16)
        own = pl.ds(each * part, each)
        write = pltpu.make_async_copy(o_ref.at[own], o_hbm.at[own], out_sems.at[part])
        write.start()
        writes.append(write)
    for write in writes:
        write.wait()


def pack(queries, keys, values, rates_t):
    rows, width = queries.shape
    heads = width // HDIM
    return pl.pallas_call(
        pack_body,
        in_specs=[pl.BlockSpec(memory_space=pl.ANY)] * 4,
        out_specs=pl.BlockSpec(memory_space=pl.ANY),
        out_shape=jax.ShapeDtypeStruct((heads, rows + 24, LANES), bf16),
        scratch_shapes=[
            pltpu.VMEM((rows, width), bf16),
            pltpu.VMEM((rows, width), bf16),
            pltpu.VMEM((rows, width), bf16),
            pltpu.VMEM((heads, rows), bf16),
            pltpu.VMEM((heads, rows + 24, LANES), bf16),
            pltpu.VMEM((heads, LANES), f32),
            pltpu.SemaphoreType.DMA((PACK_PARTS, 4)),
            pltpu.SemaphoreType.DMA((PACK_PARTS,)),
        ],
        compiler_params=pltpu.CompilerParams(vmem_limit_bytes=PACK_LIMIT),
        name="pack",
    )(queries, keys, values, rates_t)


def packed(x):
    hi, lo = split(x)
    return jnp.where(lanes_left(x.shape[0]), hi.astype(f32), lo.astype(f32)).astype(bf16)


def twice(p):
    return jnp.concatenate([p, p], axis=1)


def four(hi, lo):
    return jnp.concatenate([hi, hi, lo, lo], axis=0)


def doubled_eye():
    row = lax.broadcasted_iota(jnp.int32, (HDIM, LANES), 0)
    col = lax.broadcasted_iota(jnp.int32, (HDIM, LANES), 1)
    return jnp.where(row == lax.rem(col, HDIM), 1.0, 0.0).astype(f32)


def norm_sums():
    row = lax.broadcasted_iota(jnp.int32, (2 * LANES, 2 * LANES), 0)
    col = lax.broadcasted_iota(jnp.int32, (2 * LANES, 2 * LANES), 1)
    is_key_row = lax.rem(row, LANES) >= HDIM
    return jnp.where(is_key_row == (col < LANES), 1.0, 0.0).astype(bf16)


def inverse_norms(qk, sums):
    hi, lo = split(qk * qk)
    return lax.rsqrt(mm(jnp.concatenate([hi, lo], axis=1), sums) + 1e-06)


def attend_body(
    tv_ref, me_ref, recv_ref, msg_ref, qk_ref, ar_ref, g_ref,
    qk_scr, v_scr, r_scr, inv_scr, rate_scr, k2_scr, qs_scr, tf_scr, tb_scr, da_scr, ckh_scr, ckl_scr, h_scr,
):
    groups, rows, _ = recv_ref.shape
    toks = rows - 24
    late = toks - 24
    seglen = groups * toks
    chunks = seglen // GROUP
    blocks = seglen // QROWS
    valid = tv_ref[0]
    me = me_ref[0]

    pick = lax.broadcasted_iota(jnp.int32, (toks, LANES), 0) == lax.broadcasted_iota(jnp.int32, (toks, LANES), 1)
    left24, left_late = lanes_left(24), lanes_left(late)
    for g in range(groups):
        block = recv_ref[g].astype(f32)
        base = toks * g
        qk_scr[base : base + toks] = block[0:toks]
        tail = block[toks : toks + 24]
        tail_sw = swap_halves(tail)
        v_scr[base : base + 24] = jnp.where(left24, tail_sw, tail)
        v_scr[base + 24 : base + toks] = jnp.where(left_late, tail[0:late], tail_sw[0:late])
        r_scr[base : base + toks] = jnp.where(pick, tail[late : late + 1], 0.0)

    sums = norm_sums()
    ones = jnp.ones((LANES, LANES), bf16)
    left = lanes_left(QROWS)

    for b in range(blocks):
        at = slice(QROWS * b, QROWS * (b + 1))
        inv_scr[at] = inverse_norms(qk_scr[at], sums)[:, 0:LANES]
        rate = mm(r_scr[at].astype(bf16), ones)
        if QROWS * b < TEXT:
            position = QROWS * b + lax.broadcasted_iota(jnp.int32, (QROWS, LANES), 0)
            rate = jnp.where((position >= TEXT) | (position < valid), rate, 0.0)
        rate_scr[at] = rate
    for b in range(blocks):
        at = slice(QROWS * b, QROWS * (b + 1))
        qk = qk_scr[at]
        kq = swap_halves(qk)
        k2 = jnp.where(left, kq, qk)
        k2_scr[at] = k2.astype(bf16)
        qk_ref[at] = qk.astype(bf16)
        qs_scr[at] = jnp.where(left, qk * (1.0 / math.sqrt(HDIM)), 0.0).astype(bf16)
        inv_k = inv_scr[at]
        step = rate_scr[at] * inv_k
        inv_scr[at] = step
        ck_hi, ck_lo = split(step * inv_k * k2)
        ckh_scr[at] = ck_hi
        ckl_scr[at] = ck_lo
    for n in range(chunks):
        at = slice(GROUP * n, GROUP * (n + 1))
        k = k2_scr[at, 0:HDIM]
        gram = mm_tn(jnp.concatenate([k, k], axis=0), jnp.concatenate([ckh_scr[at], ckl_scr[at]], axis=0))
        g_hi, g_lo = split(gram)
        g_ref[n, 0:HDIM] = g_hi
        g_ref[n, HDIM : 2 * HDIM] = g_lo

    v2 = v_scr[...].astype(bf16)
    eye = doubled_eye()
    t_f, t_b = eye, eye

    def gram_right(n):
        return four(g_ref[n, 0:HDIM], g_ref[n, HDIM : 2 * HDIM])

    for m in range(chunks // 2):
        g0, g1 = (g_ref[2 * m + i, 0:HDIM].astype(f32) + g_ref[2 * m + i, HDIM : 2 * HDIM].astype(f32) for i in (0, 1))
        pair = g0 + g1 - mm(twice(packed(g0)), gram_right(2 * m + 1))
        hi, lo = split(pair)
        h_scr[m, 0:HDIM] = hi
        h_scr[m, HDIM : 2 * HDIM] = lo

    def advance_f(t, m):
        p = packed(t)
        keep(tf_scr, 2 * m, p)
        keep(tf_scr, 2 * m + 1, packed(t - mm(twice(p), gram_right(2 * m))))
        return t - mm(twice(p), four(h_scr[m, 0:HDIM], h_scr[m, HDIM : 2 * HDIM]))

    def advance_b(t, m):
        p = packed(t)
        keep(tb_scr, 2 * m + 1, p)
        keep(tb_scr, 2 * m, packed(t - mm(twice(p), gram_right(2 * m + 1))))
        hi, lo = h_scr[m, 0:HDIM], h_scr[m, HDIM : 2 * HDIM]
        row = jnp.concatenate([hi, lo], axis=1)
        return t - mm_nt(twice(p), jnp.concatenate([row, row], axis=0))

    def keep(ref, n, p):
        ref[GROUP * n : GROUP * (n + 1)] = p

    parts = seglen // AROWS
    cols = lax.broadcasted_iota(jnp.int32, (AROWS, TEXT), 1)
    left_part = lanes_left(AROWS)

    def scores_of(b):
        scores = mm_nt(qs_scr[AROWS * b : AROWS * (b + 1)], k2_scr[...])
        return jnp.concatenate([jnp.where(cols < valid, scores[:, 0:TEXT], -1e30), scores[:, TEXT:]], axis=1)

    scores = scores_of(0)
    for b in range(parts):
        at = slice(AROWS * b, AROWS * (b + 1))
        following = scores_of(b + 1) if b + 1 < parts else None
        for m in range(chunks // 2 * b // parts, chunks // 2 * (b + 1) // parts):
            t_f = advance_f(t_f, m)
            t_b = advance_b(t_b, chunks // 2 - 1 - m)
        peak = jnp.max(scores, axis=1, keepdims=True)
        raised = jnp.exp(scores - peak)
        row_total = jnp.sum(raised, axis=1, keepdims=True)
        att = (mm(raised.astype(bf16), v2) / row_total).astype(bf16).astype(f32)
        ar_ref[at] = jnp.where(left_part, att, rate_scr[at]).astype(bf16)
        da_scr[at] = packed(inv_scr[at] * att)
        scores = following

    total = jnp.zeros((LANES, 2 * LANES), f32)
    for b in range(blocks):
        reach = []
        for n in range(QROWS // GROUP * b, QROWS // GROUP * (b + 1)):
            at = slice(GROUP * n, GROUP * (n + 1))
            hi, lo = split(mm_nt(k2_scr[at], jnp.concatenate([tf_scr[at], tb_scr[at]], axis=0)))
            reach.append(jnp.concatenate([hi, lo], axis=1))
        at = slice(QROWS * b, QROWS * (b + 1))
        total = total + mm_tn(da_scr[at], jnp.concatenate(reach, axis=0))
    total = total[0:HDIM] + total[HDIM : 2 * HDIM]
    shift_f = total[:, 0:LANES] + total[:, LANES : 2 * LANES]
    shift_b = swap_halves(shift_f)
    left64 = lanes_left(HDIM)
    later = jnp.where(left64, t_f - eye, shift_f)
    earlier = jnp.where(left64, t_b - eye, shift_b)
    for s in range(msg_ref.shape[0]):
        msg_ref[s] = jnp.where(s > me, later, earlier).astype(msg_ref.dtype)


def attend(text_valid, me, received, segments, link):
    groups, rows, _ = received.shape
    seglen = groups * (rows - 24)
    chunks = seglen // GROUP
    smem = pl.BlockSpec(memory_space=pltpu.SMEM)
    vmem = pl.BlockSpec(memory_space=pltpu.VMEM)
    tall = (seglen, LANES)
    return pl.pallas_call(
        attend_body,
        in_specs=[smem, smem, vmem],
        out_specs=[vmem] * 4,
        out_shape=[jax.ShapeDtypeStruct((segments, HDIM, LANES), link)]
        + [jax.ShapeDtypeStruct(tall, bf16)] * 2
        + [jax.ShapeDtypeStruct((chunks, LANES, LANES), bf16)],
        scratch_shapes=[
            *[pltpu.VMEM(tall, f32)] * 5, *[pltpu.VMEM(tall, bf16)] * 7, pltpu.VMEM((chunks // 2, LANES, LANES), bf16),
        ],
        compiler_params=pltpu.CompilerParams(vmem_limit_bytes=VMEM_LIMIT),
        name="attend",
    )(text_valid, me, received)


def operators_body(
    qk_ref, ar_ref, g_ref, base_ref, ehi_ref, elo_ref,
    opf_scr, opb_scr, xf_scr, xb_scr, shift_scr, yhi_scr, ylo_scr, k2_scr, q2_scr, inv_scr,
):
    chunks = g_ref.shape[0]
    row_id = lax.broadcasted_iota(jnp.int32, (GROUP, LANES), 0)
    col_id = lax.rem(lax.broadcasted_iota(jnp.int32, (GROUP, LANES), 1), GROUP)
    left = lanes_left(GROUP)
    sums = norm_sums()
    eye = doubled_eye()
    x_f = jnp.concatenate([eye, jnp.zeros_like(eye)], axis=0)
    x_b = x_f

    def rows_of(n):
        return slice(GROUP * n, GROUP * (n + 1))

    def halves(x):
        x = x.astype(f32)
        x_sw = swap_halves(x)
        on_left = lanes_left(x.shape[0])
        return jnp.where(on_left, x, x_sw), jnp.where(on_left, x_sw, x)

    def advance(x, n, keep_ref):
        hi, lo = split(x)
        keep_ref[n] = jnp.concatenate([hi, lo], axis=1)
        p = jnp.where(lanes_left(2 * HDIM), hi.astype(f32), lo.astype(f32)).astype(bf16)
        x = x - mm(twice(p), four(g_ref[n, 0:HDIM], g_ref[n, HDIM : 2 * HDIM]))
        return jnp.concatenate([x[0:HDIM], x[HDIM : 2 * HDIM] + shift_scr[n]], axis=0)

    blocks = chunks * GROUP // QROWS
    for b in range(blocks):
        at = slice(QROWS * b, QROWS * (b + 1))
        inv_scr[at] = inverse_norms(qk_ref[at].astype(f32), sums)
    for b in range(blocks):
        at = slice(QROWS * b, QROWS * (b + 1))
        inv_k = inv_scr[at, 0:LANES]
        q2, k2 = halves(qk_ref[at])
        att, rate = halves(ar_ref[at])
        step = rate * inv_k
        ck_hi, ck_lo = split(step * inv_k * k2)
        da_hi, da_lo = split(step * att)
        yhi_scr[at] = jnp.concatenate([ck_hi, da_hi], axis=1)
        ylo_scr[at] = jnp.concatenate([ck_lo, da_lo], axis=1)
        base_ref[at] = att
        q2_scr[at] = q2.astype(bf16)
        k2_scr[at] = k2.astype(bf16)
    for n in range(chunks):
        at = rows_of(n)
        k2 = k2_scr[at]
        da = jnp.concatenate([yhi_scr[at, LANES : LANES + HDIM], ylo_scr[at, LANES : LANES + HDIM]], axis=0)
        shift_scr[n] = mm_tn(da, jnp.concatenate([k2, k2], axis=0))

    for n in range(chunks):
        x_f = advance(x_f, n, xf_scr)
        x_b = advance(x_b, chunks - 1 - n, xb_scr)
        at = rows_of(n)
        q2, k2 = q2_scr[at].astype(f32), k2_scr[at]
        scores = mm_nt(jnp.where(left, q2, 0.0).astype(bf16), jnp.concatenate([k2, k2], axis=0))
        both = packed(
            jnp.concatenate(
                [jnp.where(col_id <= row_id, scores, 0.0), jnp.where(col_id >= row_id, scores, 0.0)], axis=0
            )
        )
        y_hi, y_lo = yhi_scr[at], ylo_scr[at]
        pushed = mm(twice(both), four(y_hi, y_lo))
        scale = math.sqrt(HDIM) * inv_scr[at, LANES : 2 * LANES]
        opf_scr[at] = packed(scale * (q2 - pushed[0:GROUP, 0:LANES]))
        opb_scr[at] = packed(scale * (q2 - pushed[GROUP : 2 * GROUP, 0:LANES]))
        base_ref[at] = base_ref[at] + scale * (
            pushed[0:GROUP, LANES : 2 * LANES] + pushed[GROUP : 2 * GROUP, LANES : 2 * LANES]
        )

    for n in range(chunks):
        at = rows_of(n)

        def through(op_ref, x_ref):
            t, w = x_ref[n, 0:HDIM], x_ref[n, HDIM : 2 * HDIM]
            return mm_nt(twice(op_ref[at]), jnp.concatenate([t, t, w, w], axis=0))

        from_f, from_b = through(opf_scr, xf_scr), through(opb_scr, xb_scr)
        base_ref[at] = base_ref[at] + from_f[:, LANES : 2 * LANES] + from_b[:, LANES : 2 * LANES]
        e_hi, e_lo = split(jnp.where(left, from_f[:, 0:LANES], from_b[:, 0:LANES]))
        ehi_ref[at] = e_hi
        elo_ref[at] = e_lo


def operators(*held):
    tall = held[0].shape
    chunks = tall[0] // GROUP
    state = (chunks, 2 * HDIM, 2 * LANES)
    return pl.pallas_call(
        operators_body,
        out_shape=[
            jax.ShapeDtypeStruct(tall, f32),
            jax.ShapeDtypeStruct(tall, bf16),
            jax.ShapeDtypeStruct(tall, bf16),
        ],
        scratch_shapes=[
            pltpu.VMEM(tall, bf16), pltpu.VMEM(tall, bf16), pltpu.VMEM(state, bf16), pltpu.VMEM(state, bf16),
            pltpu.VMEM((chunks, HDIM, LANES), f32),
            pltpu.VMEM((tall[0], 2 * LANES), bf16), pltpu.VMEM((tall[0], 2 * LANES), bf16),
            pltpu.VMEM(tall, bf16), pltpu.VMEM(tall, bf16), pltpu.VMEM((tall[0], 2 * LANES), f32),
        ],
        compiler_params=pltpu.CompilerParams(vmem_limit_bytes=VMEM_LIMIT),
        cost_estimate=pl.CostEstimate(flops=2_000_000_000, bytes_accessed=8_000_000, transcendentals=0),
        name="operators",
    )(*held)


def finish_body(me_ref, msg_ref, sf_ref, sb_ref, base_ref, ehi_ref, elo_ref, out_ref, scr):
    segments = msg_ref.shape[0]
    groups, half, _ = out_ref.shape
    me = me_ref[0]
    left64 = lanes_left(HDIM)

    def doubled_transpose(state):
        return jnp.concatenate([state, state], axis=0).T

    def times(x, decay):
        return mm(twice(packed(x)), four(*split(decay)))

    def leaf(i):
        m = msg_ref[i].astype(f32)
        m_sw = swap_halves(m)
        return jnp.concatenate([jnp.where(left64, m, m_sw), jnp.where(left64, m_sw, m)], axis=0)

    def then(first, second):
        return first + second + times(first, second[0:HDIM])

    def sibling(level):
        size = 2**level
        block = lax.div(me, size)
        before = lax.rem(block, 2) == 1
        start = jnp.where(before, block - 1, block + 1) * size
        nodes = [leaf(start + jnp.where(before, i, size - 1 - i)) for i in range(size)]
        while len(nodes) > 1:
            nodes = [then(nodes[i], nodes[i + 1]) for i in range(0, len(nodes), 2)]
        return before, nodes[0]

    w_f, w_b = doubled_transpose(sf_ref[0]), doubled_transpose(sb_ref[0])
    for before, node in [sibling(level) for level in reversed(range(segments.bit_length() - 1))]:
        state = jnp.where(before, w_f, w_b)
        state = state + times(state, node[0:HDIM]) + node[HDIM : 2 * HDIM]
        w_f, w_b = jnp.where(before, state, w_f), jnp.where(before, w_b, state)
    w_hi, w_lo = split(jnp.where(left64, w_f, w_b))
    w_row = jnp.concatenate([w_hi, w_hi, w_lo], axis=1)
    e_hi = ehi_ref[...]
    got = mm_nt(jnp.concatenate([e_hi, elo_ref[...], e_hi], axis=1), jnp.concatenate([w_row, w_row], axis=0))
    scr[...] = got + base_ref[...]
    left = lanes_left(half)
    for g in range(groups):
        first = scr[2 * half * g : 2 * half * g + half]
        second = scr[2 * half * g + half : 2 * half * (g + 1)]
        out_ref[g] = jnp.where(left, first, second).astype(bf16)


def finish(me, maps, state_fwd, state_bwd, base, ehi, elo, groups):
    seglen = base.shape[0]
    half = seglen // groups // 2
    smem = pl.BlockSpec(memory_space=pltpu.SMEM)
    vmem = pl.BlockSpec(memory_space=pltpu.VMEM)
    return pl.pallas_call(
        finish_body,
        in_specs=[smem] + [vmem] * 6,
        out_specs=vmem,
        out_shape=jax.ShapeDtypeStruct((groups, half, LANES), bf16),
        scratch_shapes=[pltpu.VMEM((seglen, LANES), f32)],
        compiler_params=pltpu.CompilerParams(vmem_limit_bytes=VMEM_LIMIT),
        name="finish",
    )(me, maps, state_fwd, state_bwd, base, ehi, elo)


def unpack_body(x_ref, out_ref, scr):
    heads, half, _ = x_ref.shape
    left = lanes_left(half)
    for p in range(heads // 2):
        even = x_ref[2 * p].astype(f32)
        odd = x_ref[2 * p + 1].astype(f32)
        scr[0:half] = jnp.where(left, even, swap_halves(odd))
        scr[half : 2 * half] = jnp.where(left, swap_halves(even), odd)
        out_ref[:, LANES * p : LANES * (p + 1)] = scr[...].astype(bf16)


def unpack(x):
    heads, half, _ = x.shape
    return pl.pallas_call(
        unpack_body,
        out_shape=jax.ShapeDtypeStruct((2 * half, heads * HDIM), bf16),
        scratch_shapes=[pltpu.VMEM((2 * half, LANES), f32)],
        compiler_params=pltpu.CompilerParams(vmem_limit_bytes=VMEM_LIMIT),
        name="unpack",
    )(x)


def exchange(x, axis):
    return lax.all_to_all(x, axis, split_axis=0, concat_axis=0, tiled=True)


def local(queries, keys, values, rates, text_valid, state_fwd, state_bwd):
    segments = lax.axis_size("seg")
    groups = lax.axis_size("grp")
    me = lax.axis_index("seg").astype(jnp.int32).reshape(1)
    received = exchange(pack(queries, keys, values, rates.T), "grp")
    msg, *held = attend(text_valid, me, received, segments, bf16)
    maps = exchange(msg, "seg")
    base, ehi, elo = operators(*held)
    mixed = finish(me, maps, state_fwd, state_bwd, base, ehi, elo, groups)
    return unpack(exchange(mixed, "grp"))


def solution(mesh):
    in_specs = (
        P(("seg", "grp"), None),
        P(("seg", "grp"), None),
        P(("seg", "grp"), None),
        P(("seg", "grp"), None),
        P("seg"),
        P("grp", None, None),
        P("grp", None, None),
    )
    out_specs = P(("seg", "grp"), None)
    return jax.shard_map(local, mesh=mesh, in_specs=in_specs, out_specs=out_specs, check_vma=False)
```

```python
import math

import jax
import jax.numpy as jnp
from jax import lax
from jax.experimental import pallas as pl
from jax.experimental.pallas import tpu as pltpu
from jax.sharding import PartitionSpec as P

GROUP = 64
TEXT = 128
HDIM = 64
LANES = 128
QROWS = 256
AROWS = 128
PACK_PARTS = 2
VMEM_LIMIT = 24 * 1024 * 1024
PACK_LIMIT = 62 * 1024 * 1024

bf16 = jnp.bfloat16
f32 = jnp.float32


def split(x):
    hi = x.astype(bf16)
    return hi, (x - hi.astype(f32)).astype(bf16)


def mm(a, b):
    return lax.dot_general(a, b, (((1,), (0,)), ((), ())), preferred_element_type=f32)


def mm_nt(a, b):
    return lax.dot_general(a, b, (((1,), (1,)), ((), ())), preferred_element_type=f32)


def mm_tn(a, b):
    return lax.dot_general(a, b, (((0,), (0,)), ((), ())), preferred_element_type=f32)


def lanes_left(rows):
    return lax.broadcasted_iota(jnp.int32, (rows, LANES), 1) < HDIM


def swap_halves(x):
    return pltpu.roll(x, HDIM, 1)


def pack_body(q_hbm, k_hbm, v_hbm, r_hbm, o_hbm, q_ref, k_ref, v_ref, r_ref, o_ref, rate_scr, in_sems, out_sems):
    rows, width = q_ref.shape
    heads = width // HDIM
    late = rows - 24
    parts = in_sems.shape[0]
    wide = width // parts
    each = heads // parts
    rate_copy = pltpu.make_async_copy(r_hbm, r_ref, in_sems.at[0, 3])
    rate_copy.start()
    reads, writes = [], []
    for part in range(parts):
        cols = pl.ds(wide * part, wide)
        reads.append(
            [
                pltpu.make_async_copy(source.at[:, cols], target.at[:, cols], in_sems.at[part, i])
                for i, (source, target) in enumerate(((q_hbm, q_ref), (k_hbm, k_ref), (v_hbm, v_ref)))
            ]
        )
        for read in reads[part]:
            read.start()
    left = lanes_left(rows)
    left24 = lanes_left(24)
    rate_scr[...] = jnp.zeros_like(rate_scr)
    rate_copy.wait()
    rate_scr[:, 0:rows] = r_ref[...].astype(f32)
    for part in range(parts):
        for read in reads[part]:
            read.wait()
        for p in range(each // 2 * part, each // 2 * (part + 1)):
            cols = slice(LANES * p, LANES * (p + 1))
            q = q_ref[:, cols].astype(f32)
            k = k_ref[:, cols].astype(f32)
            v = v_ref[:, cols].astype(f32)
            q_sw, k_sw, v_sw = swap_halves(q), swap_halves(k), swap_halves(v)
            for odd in (0, 1):
                head = 2 * p + odd
                qk = jnp.where(left, q_sw, k) if odd else jnp.where(left, q, k_sw)
                v_right, v_left = (v, v_sw) if odd else (v_sw, v)
                rate = jnp.broadcast_to(rate_scr[head : head + 1, :], (24 - late, LANES))
                low = jnp.concatenate([v_left[24:rows], rate], axis=0)
                vr = jnp.where(left24, low, v_right[0:24])
                o_ref[head] = jnp.concatenate([qk, vr], axis=0).astype(bf16)
        own = pl.ds(each * part, each)
        write = pltpu.make_async_copy(o_ref.at[own], o_hbm.at[own], out_sems.at[part])
        write.start()
        writes.append(write)
    for write in writes:
        write.wait()


def pack(queries, keys, values, rates_t):
    rows, width = queries.shape
    heads = width // HDIM
    return pl.pallas_call(
        pack_body,
        in_specs=[pl.BlockSpec(memory_space=pl.ANY)] * 4,
        out_specs=pl.BlockSpec(memory_space=pl.ANY),
        out_shape=jax.ShapeDtypeStruct((heads, rows + 24, LANES), bf16),
        scratch_shapes=[
            pltpu.VMEM((rows, width), bf16),
            pltpu.VMEM((rows, width), bf16),
            pltpu.VMEM((rows, width), bf16),
            pltpu.VMEM((heads, rows), bf16),
            pltpu.VMEM((heads, rows + 24, LANES), bf16),
            pltpu.VMEM((heads, LANES), f32),
            pltpu.SemaphoreType.DMA((PACK_PARTS, 4)),
            pltpu.SemaphoreType.DMA((PACK_PARTS,)),
        ],
        compiler_params=pltpu.CompilerParams(vmem_limit_bytes=PACK_LIMIT),
        name="pack",
    )(queries, keys, values, rates_t)


def packed(x):
    hi, lo = split(x)
    return jnp.where(lanes_left(x.shape[0]), hi.astype(f32), lo.astype(f32)).astype(bf16)


def twice(p):
    return jnp.concatenate([p, p], axis=1)


def four(hi, lo):
    return jnp.concatenate([hi, hi, lo, lo], axis=0)


def doubled_eye():
    row = lax.broadcasted_iota(jnp.int32, (HDIM, LANES), 0)
    col = lax.broadcasted_iota(jnp.int32, (HDIM, LANES), 1)
    return jnp.where(row == lax.rem(col, HDIM), 1.0, 0.0).astype(f32)


def norm_sums():
    row = lax.broadcasted_iota(jnp.int32, (2 * LANES, 2 * LANES), 0)
    col = lax.broadcasted_iota(jnp.int32, (2 * LANES, 2 * LANES), 1)
    is_key_row = lax.rem(row, LANES) >= HDIM
    return jnp.where(is_key_row == (col < LANES), 1.0, 0.0).astype(bf16)


def inverse_norms(qk, sums):
    hi, lo = split(qk * qk)
    return lax.rsqrt(mm(jnp.concatenate([hi, lo], axis=1), sums) + 1e-06)


def attend_body(
    tv_ref, me_ref, recv_ref, msg_ref, qk_ref, ar_ref, g_ref,
    qk_scr, v_scr, r_scr, inv_scr, rate_scr, k2_scr, qs_scr, tf_scr, tb_scr, da_scr, ckh_scr, ckl_scr, h_scr, reach_scr,
):
    groups, rows, _ = recv_ref.shape
    toks = rows - 24
    late = toks - 24
    seglen = groups * toks
    chunks = seglen // GROUP
    blocks = seglen // QROWS
    valid = tv_ref[0]
    me = me_ref[0]

    pick = lax.broadcasted_iota(jnp.int32, (toks, LANES), 0) == lax.broadcasted_iota(jnp.int32, (toks, LANES), 1)
    left24, left_late = lanes_left(24), lanes_left(late)
    for g in range(groups):
        block = recv_ref[g].astype(f32)
        base = toks * g
        qk_scr[base : base + toks] = block[0:toks]
        tail = block[toks : toks + 24]
        tail_sw = swap_halves(tail)
        v_scr[base : base + 24] = jnp.where(left24, tail_sw, tail)
        v_scr[base + 24 : base + toks] = jnp.where(left_late, tail[0:late], tail_sw[0:late])
        r_scr[base : base + toks] = jnp.where(pick, tail[late : late + 1], 0.0)

    sums = norm_sums()
    ones = jnp.ones((LANES, LANES), bf16)
    left = lanes_left(QROWS)

    for b in range(blocks):
        at = slice(QROWS * b, QROWS * (b + 1))
        inv_scr[at] = inverse_norms(qk_scr[at], sums)[:, 0:LANES]
        rate = mm(r_scr[at].astype(bf16), ones)
        if QROWS * b < TEXT:
            position = QROWS * b + lax.broadcasted_iota(jnp.int32, (QROWS, LANES), 0)
            rate = jnp.where((position >= TEXT) | (position < valid), rate, 0.0)
        rate_scr[at] = rate
    for b in range(blocks):
        at = slice(QROWS * b, QROWS * (b + 1))
        qk = qk_scr[at]
        kq = swap_halves(qk)
        k2 = jnp.where(left, kq, qk)
        k2_scr[at] = k2.astype(bf16)
        qk_ref[at] = qk.astype(bf16)
        qs_scr[at] = jnp.where(left, qk * (1.0 / math.sqrt(HDIM)), 0.0).astype(bf16)
        inv_k = inv_scr[at]
        step = rate_scr[at] * inv_k
        inv_scr[at] = step
        ck_hi, ck_lo = split(step * inv_k * k2)
        ckh_scr[at] = ck_hi
        ckl_scr[at] = ck_lo
    for n in range(chunks):
        at = slice(GROUP * n, GROUP * (n + 1))
        k = k2_scr[at, 0:HDIM]
        gram = mm_tn(jnp.concatenate([k, k], axis=0), jnp.concatenate([ckh_scr[at], ckl_scr[at]], axis=0))
        g_hi, g_lo = split(gram)
        g_ref[n, 0:HDIM] = g_hi
        g_ref[n, HDIM : 2 * HDIM] = g_lo

    v2 = v_scr[...].astype(bf16)
    eye = doubled_eye()
    t_f, t_b = eye, eye

    def gram_right(n):
        return four(g_ref[n, 0:HDIM], g_ref[n, HDIM : 2 * HDIM])

    for m in range(chunks // 2):
        g0, g1 = (g_ref[2 * m + i, 0:HDIM].astype(f32) + g_ref[2 * m + i, HDIM : 2 * HDIM].astype(f32) for i in (0, 1))
        pair = g0 + g1 - mm(twice(packed(g0)), gram_right(2 * m + 1))
        hi, lo = split(pair)
        h_scr[m, 0:HDIM] = hi
        h_scr[m, HDIM : 2 * HDIM] = lo

    def advance_f(t, m):
        p = packed(t)
        keep(tf_scr, 2 * m, p)
        keep(tf_scr, 2 * m + 1, packed(t - mm(twice(p), gram_right(2 * m))))
        return t - mm(twice(p), four(h_scr[m, 0:HDIM], h_scr[m, HDIM : 2 * HDIM]))

    def advance_b(t, m):
        p = packed(t)
        keep(tb_scr, 2 * m + 1, p)
        keep(tb_scr, 2 * m, packed(t - mm(twice(p), gram_right(2 * m + 1))))
        hi, lo = h_scr[m, 0:HDIM], h_scr[m, HDIM : 2 * HDIM]
        row = jnp.concatenate([hi, lo], axis=1)
        return t - mm_nt(twice(p), jnp.concatenate([row, row], axis=0))

    def keep(ref, n, p):
        ref[GROUP * n : GROUP * (n + 1)] = p

    parts = seglen // AROWS
    cols = lax.broadcasted_iota(jnp.int32, (AROWS, TEXT), 1)
    left_part = lanes_left(AROWS)

    def scores_of(b):
        scores = mm_nt(qs_scr[AROWS * b : AROWS * (b + 1)], k2_scr[...])
        return jnp.concatenate([jnp.where(cols < valid, scores[:, 0:TEXT], -1e30), scores[:, TEXT:]], axis=1)

    def close(b, raised, row_total):
        at = slice(AROWS * b, AROWS * (b + 1))
        att = (mm(raised, v2) / row_total).astype(bf16).astype(f32)
        ar_ref[at] = jnp.where(left_part, att, rate_scr[at]).astype(bf16)
        da_scr[at] = packed(inv_scr[at] * att)

    scores = scores_of(0)
    for b in range(parts):
        if b:
            close(b - 1, raised, row_total)
        following = scores_of(b + 1) if b + 1 < parts else None
        for m in range(chunks // 2 * b // parts, chunks // 2 * (b + 1) // parts):
            t_f = advance_f(t_f, m)
            t_b = advance_b(t_b, chunks // 2 - 1 - m)
        peak = jnp.max(scores, axis=1, keepdims=True)
        raised = jnp.exp(scores - peak)
        row_total = jnp.sum(raised, axis=1, keepdims=True)
        raised = raised.astype(bf16)
        scores = following
    close(parts - 1, raised, row_total)

    for n in range(chunks):
        at = slice(GROUP * n, GROUP * (n + 1))
        hi, lo = split(mm_nt(k2_scr[at], jnp.concatenate([tf_scr[at], tb_scr[at]], axis=0)))
        reach_scr[at] = jnp.concatenate([hi, lo], axis=1)
    total = mm_tn(da_scr[...], reach_scr[...])
    total = total[0:HDIM] + total[HDIM : 2 * HDIM]
    shift_f = total[:, 0:LANES] + total[:, LANES : 2 * LANES]
    shift_b = swap_halves(shift_f)
    left64 = lanes_left(HDIM)
    later = jnp.where(left64, t_f - eye, shift_f)
    earlier = jnp.where(left64, t_b - eye, shift_b)
    for s in range(msg_ref.shape[0]):
        msg_ref[s] = jnp.where(s > me, later, earlier).astype(msg_ref.dtype)


def attend(text_valid, me, received, segments, link):
    groups, rows, _ = received.shape
    seglen = groups * (rows - 24)
    chunks = seglen // GROUP
    smem = pl.BlockSpec(memory_space=pltpu.SMEM)
    vmem = pl.BlockSpec(memory_space=pltpu.VMEM)
    tall = (seglen, LANES)
    return pl.pallas_call(
        attend_body,
        in_specs=[smem, smem, vmem],
        out_specs=[vmem] * 4,
        out_shape=[jax.ShapeDtypeStruct((segments, HDIM, LANES), link)]
        + [jax.ShapeDtypeStruct(tall, bf16)] * 2
        + [jax.ShapeDtypeStruct((chunks, LANES, LANES), bf16)],
        scratch_shapes=[
            *[pltpu.VMEM(tall, f32)] * 5, *[pltpu.VMEM(tall, bf16)] * 7, pltpu.VMEM((chunks // 2, LANES, LANES), bf16),
            pltpu.VMEM((seglen, 2 * LANES), bf16),
        ],
        compiler_params=pltpu.CompilerParams(vmem_limit_bytes=VMEM_LIMIT),
        name="attend",
    )(text_valid, me, received)


def operators_body(
    qk_ref, ar_ref, g_ref, base_ref, ehi_ref, elo_ref,
    opf_scr, opb_scr, xf_scr, xb_scr, shift_scr, yhi_scr, ylo_scr, k2_scr, q2_scr, inv_scr,
):
    chunks = g_ref.shape[0]
    row_id = lax.broadcasted_iota(jnp.int32, (GROUP, LANES), 0)
    col_id = lax.rem(lax.broadcasted_iota(jnp.int32, (GROUP, LANES), 1), GROUP)
    left = lanes_left(GROUP)
    sums = norm_sums()
    eye = doubled_eye()
    x_f = jnp.concatenate([eye, jnp.zeros_like(eye)], axis=0)
    x_b = x_f

    def rows_of(n):
        return slice(GROUP * n, GROUP * (n + 1))

    def halves(x):
        x = x.astype(f32)
        x_sw = swap_halves(x)
        on_left = lanes_left(x.shape[0])
        return jnp.where(on_left, x, x_sw), jnp.where(on_left, x_sw, x)

    def advance(x, n, keep_ref):
        hi, lo = split(x)
        keep_ref[n] = jnp.concatenate([hi, lo], axis=1)
        p = jnp.where(lanes_left(2 * HDIM), hi.astype(f32), lo.astype(f32)).astype(bf16)
        x = x - mm(twice(p), four(g_ref[n, 0:HDIM], g_ref[n, HDIM : 2 * HDIM]))
        return jnp.concatenate([x[0:HDIM], x[HDIM : 2 * HDIM] + shift_scr[n]], axis=0)

    blocks = chunks * GROUP // QROWS
    for b in range(blocks):
        at = slice(QROWS * b, QROWS * (b + 1))
        inv_scr[at] = inverse_norms(qk_ref[at].astype(f32), sums)
    for b in range(blocks):
        at = slice(QROWS * b, QROWS * (b + 1))
        inv_k = inv_scr[at, 0:LANES]
        q2, k2 = halves(qk_ref[at])
        att, rate = halves(ar_ref[at])
        step = rate * inv_k
        ck_hi, ck_lo = split(step * inv_k * k2)
        da_hi, da_lo = split(step * att)
        yhi_scr[at] = jnp.concatenate([ck_hi, da_hi], axis=1)
        ylo_scr[at] = jnp.concatenate([ck_lo, da_lo], axis=1)
        base_ref[at] = att
        q2_scr[at] = q2.astype(bf16)
        k2_scr[at] = k2.astype(bf16)
    for n in range(chunks):
        at = rows_of(n)
        k2 = k2_scr[at]
        da = jnp.concatenate([yhi_scr[at, LANES : LANES + HDIM], ylo_scr[at, LANES : LANES + HDIM]], axis=0)
        shift_scr[n] = mm_tn(da, jnp.concatenate([k2, k2], axis=0))

    for n in range(chunks):
        x_f = advance(x_f, n, xf_scr)
        x_b = advance(x_b, chunks - 1 - n, xb_scr)
        at = rows_of(n)
        q2, k2 = q2_scr[at].astype(f32), k2_scr[at]
        scores = mm_nt(jnp.where(left, q2, 0.0).astype(bf16), jnp.concatenate([k2, k2], axis=0))
        both = packed(
            jnp.concatenate(
                [jnp.where(col_id <= row_id, scores, 0.0), jnp.where(col_id >= row_id, scores, 0.0)], axis=0
            )
        )
        y_hi, y_lo = yhi_scr[at], ylo_scr[at]
        pushed = mm(twice(both), four(y_hi, y_lo))
        scale = math.sqrt(HDIM) * inv_scr[at, LANES : 2 * LANES]
        opf_scr[at] = packed(scale * (q2 - pushed[0:GROUP, 0:LANES]))
        opb_scr[at] = packed(scale * (q2 - pushed[GROUP : 2 * GROUP, 0:LANES]))
        base_ref[at] = base_ref[at] + scale * (
            pushed[0:GROUP, LANES : 2 * LANES] + pushed[GROUP : 2 * GROUP, LANES : 2 * LANES]
        )

    for n in range(chunks):
        at = rows_of(n)

        def through(op_ref, x_ref):
            t, w = x_ref[n, 0:HDIM], x_ref[n, HDIM : 2 * HDIM]
            return mm_nt(twice(op_ref[at]), jnp.concatenate([t, t, w, w], axis=0))

        from_f, from_b = through(opf_scr, xf_scr), through(opb_scr, xb_scr)
        base_ref[at] = base_ref[at] + from_f[:, LANES : 2 * LANES] + from_b[:, LANES : 2 * LANES]
        e_hi, e_lo = split(jnp.where(left, from_f[:, 0:LANES], from_b[:, 0:LANES]))
        ehi_ref[at] = e_hi
        elo_ref[at] = e_lo


def operators(*held):
    tall = held[0].shape
    chunks = tall[0] // GROUP
    state = (chunks, 2 * HDIM, 2 * LANES)
    return pl.pallas_call(
        operators_body,
        out_shape=[
            jax.ShapeDtypeStruct(tall, f32),
            jax.ShapeDtypeStruct(tall, bf16),
            jax.ShapeDtypeStruct(tall, bf16),
        ],
        scratch_shapes=[
            pltpu.VMEM(tall, bf16), pltpu.VMEM(tall, bf16), pltpu.VMEM(state, bf16), pltpu.VMEM(state, bf16),
            pltpu.VMEM((chunks, HDIM, LANES), f32),
            pltpu.VMEM((tall[0], 2 * LANES), bf16), pltpu.VMEM((tall[0], 2 * LANES), bf16),
            pltpu.VMEM(tall, bf16), pltpu.VMEM(tall, bf16), pltpu.VMEM((tall[0], 2 * LANES), f32),
        ],
        compiler_params=pltpu.CompilerParams(vmem_limit_bytes=VMEM_LIMIT),
        cost_estimate=pl.CostEstimate(flops=2_000_000_000, bytes_accessed=8_000_000, transcendentals=0),
        name="operators",
    )(*held)


def finish_body(me_ref, msg_ref, sf_ref, sb_ref, base_ref, ehi_ref, elo_ref, out_ref, scr):
    segments = msg_ref.shape[0]
    groups, half, _ = out_ref.shape
    me = me_ref[0]
    left64 = lanes_left(HDIM)

    def doubled_transpose(state):
        return jnp.concatenate([state, state], axis=0).T

    def times(x, decay):
        return mm(twice(packed(x)), four(*split(decay)))

    def times_sent(x, decay):
        decay = decay.astype(bf16)
        return mm(packed(x), jnp.concatenate([decay, decay], axis=0))

    def leaf(i):
        m = msg_ref[i].astype(f32)
        m_sw = swap_halves(m)
        return jnp.concatenate([jnp.where(left64, m, m_sw), jnp.where(left64, m_sw, m)], axis=0)

    def then(first, second, times):
        return first + second + times(first, second[0:HDIM])

    def sibling(level):
        size = 2**level
        block = lax.div(me, size)
        before = lax.rem(block, 2) == 1
        start = jnp.where(before, block - 1, block + 1) * size
        nodes = [leaf(start + jnp.where(before, i, size - 1 - i)) for i in range(size)]
        way = times_sent
        while len(nodes) > 1:
            nodes = [then(nodes[i], nodes[i + 1], way) for i in range(0, len(nodes), 2)]
            way = times
        return before, nodes[0], way

    w_f, w_b = doubled_transpose(sf_ref[0]), doubled_transpose(sb_ref[0])
    for before, node, way in [sibling(level) for level in reversed(range(segments.bit_length() - 1))]:
        state = jnp.where(before, w_f, w_b)
        state = state + way(state, node[0:HDIM]) + node[HDIM : 2 * HDIM]
        w_f, w_b = jnp.where(before, state, w_f), jnp.where(before, w_b, state)
    w_hi, w_lo = split(jnp.where(left64, w_f, w_b))
    w_row = jnp.concatenate([w_hi, w_hi, w_lo], axis=1)
    e_hi = ehi_ref[...]
    got = mm_nt(jnp.concatenate([e_hi, elo_ref[...], e_hi], axis=1), jnp.concatenate([w_row, w_row], axis=0))
    scr[...] = got + base_ref[...]
    left = lanes_left(half)
    for g in range(groups):
        first = scr[2 * half * g : 2 * half * g + half]
        second = scr[2 * half * g + half : 2 * half * (g + 1)]
        out_ref[g] = jnp.where(left, first, second).astype(bf16)


def finish(me, maps, state_fwd, state_bwd, base, ehi, elo, groups):
    seglen = base.shape[0]
    half = seglen // groups // 2
    smem = pl.BlockSpec(memory_space=pltpu.SMEM)
    vmem = pl.BlockSpec(memory_space=pltpu.VMEM)
    return pl.pallas_call(
        finish_body,
        in_specs=[smem] + [vmem] * 6,
        out_specs=vmem,
        out_shape=jax.ShapeDtypeStruct((groups, half, LANES), bf16),
        scratch_shapes=[pltpu.VMEM((seglen, LANES), f32)],
        compiler_params=pltpu.CompilerParams(vmem_limit_bytes=VMEM_LIMIT),
        name="finish",
    )(me, maps, state_fwd, state_bwd, base, ehi, elo)


def unpack_body(x_ref, out_ref, scr):
    heads, half, _ = x_ref.shape
    left = lanes_left(half)
    for p in range(heads // 2):
        even = x_ref[2 * p].astype(f32)
        odd = x_ref[2 * p + 1].astype(f32)
        scr[0:half] = jnp.where(left, even, swap_halves(odd))
        scr[half : 2 * half] = jnp.where(left, swap_halves(even), odd)
        out_ref[:, LANES * p : LANES * (p + 1)] = scr[...].astype(bf16)


def unpack(x):
    heads, half, _ = x.shape
    return pl.pallas_call(
        unpack_body,
        out_shape=jax.ShapeDtypeStruct((2 * half, heads * HDIM), bf16),
        scratch_shapes=[pltpu.VMEM((2 * half, LANES), f32)],
        compiler_params=pltpu.CompilerParams(vmem_limit_bytes=VMEM_LIMIT),
        name="unpack",
    )(x)


def exchange(x, axis):
    return lax.all_to_all(x, axis, split_axis=0, concat_axis=0, tiled=True)


def local(queries, keys, values, rates, text_valid, state_fwd, state_bwd):
    segments = lax.axis_size("seg")
    groups = lax.axis_size("grp")
    me = lax.axis_index("seg").astype(jnp.int32).reshape(1)
    received = exchange(pack(queries, keys, values, rates.T), "grp")
    msg, *held = attend(text_valid, me, received, segments, bf16)
    maps = exchange(msg, "seg")
    base, ehi, elo = operators(*held)
    mixed = finish(me, maps, state_fwd, state_bwd, base, ehi, elo, groups)
    return unpack(exchange(mixed, "grp"))


def solution(mesh):
    in_specs = (
        P(("seg", "grp"), None),
        P(("seg", "grp"), None),
        P(("seg", "grp"), None),
        P(("seg", "grp"), None),
        P("seg"),
        P("grp", None, None),
        P("grp", None, None),
    )
    out_specs = P(("seg", "grp"), None)
    return jax.shard_map(local, mesh=mesh, in_specs=in_specs, out_specs=out_specs, check_vma=False)
```

```python
import math

import jax
import jax.numpy as jnp
from jax import lax
from jax.experimental import pallas as pl
from jax.experimental.pallas import tpu as pltpu
from jax.sharding import PartitionSpec as P

GROUP = 64
TEXT = 128
HDIM = 64
LANES = 128
QROWS = 256
AROWS = 128
QUAD = 4
PACK_PARTS = 2
VMEM_LIMIT = 24 * 1024 * 1024
PACK_LIMIT = 62 * 1024 * 1024

bf16 = jnp.bfloat16
f32 = jnp.float32


def split(x):
    hi = x.astype(bf16)
    return hi, (x - hi.astype(f32)).astype(bf16)


def mm(a, b):
    return lax.dot_general(a, b, (((1,), (0,)), ((), ())), preferred_element_type=f32)


def mm_nt(a, b):
    return lax.dot_general(a, b, (((1,), (1,)), ((), ())), preferred_element_type=f32)


def mm_tn(a, b):
    return lax.dot_general(a, b, (((0,), (0,)), ((), ())), preferred_element_type=f32)


def lanes_left(rows):
    return lax.broadcasted_iota(jnp.int32, (rows, LANES), 1) < HDIM


def swap_halves(x):
    return pltpu.roll(x, HDIM, 1)


def pack_body(q_hbm, k_hbm, v_hbm, r_hbm, o_hbm, q_ref, k_ref, v_ref, r_ref, o_ref, rate_scr, in_sems, out_sems):
    rows, width = q_ref.shape
    heads = width // HDIM
    late = rows - 24
    parts = in_sems.shape[0]
    wide = width // parts
    each = heads // parts
    rate_copy = pltpu.make_async_copy(r_hbm, r_ref, in_sems.at[0, 3])
    rate_copy.start()
    reads, writes = [], []
    for part in range(parts):
        cols = pl.ds(wide * part, wide)
        reads.append(
            [
                pltpu.make_async_copy(source.at[:, cols], target.at[:, cols], in_sems.at[part, i])
                for i, (source, target) in enumerate(((q_hbm, q_ref), (k_hbm, k_ref), (v_hbm, v_ref)))
            ]
        )
        for read in reads[part]:
            read.start()
    left = lanes_left(rows)
    left24 = lanes_left(24)
    rate_scr[...] = jnp.zeros_like(rate_scr)
    rate_copy.wait()
    rate_scr[:, 0:rows] = r_ref[...].astype(f32)
    for part in range(parts):
        for read in reads[part]:
            read.wait()
        for p in range(each // 2 * part, each // 2 * (part + 1)):
            cols = slice(LANES * p, LANES * (p + 1))
            q = q_ref[:, cols].astype(f32)
            k = k_ref[:, cols].astype(f32)
            v = v_ref[:, cols].astype(f32)
            q_sw, k_sw, v_sw = swap_halves(q), swap_halves(k), swap_halves(v)
            for odd in (0, 1):
                head = 2 * p + odd
                qk = jnp.where(left, q_sw, k) if odd else jnp.where(left, q, k_sw)
                v_right, v_left = (v, v_sw) if odd else (v_sw, v)
                rate = jnp.broadcast_to(rate_scr[head : head + 1, :], (24 - late, LANES))
                low = jnp.concatenate([v_left[24:rows], rate], axis=0)
                vr = jnp.where(left24, low, v_right[0:24])
                o_ref[head] = jnp.concatenate([qk, vr], axis=0).astype(bf16)
        own = pl.ds(each * part, each)
        write = pltpu.make_async_copy(o_ref.at[own], o_hbm.at[own], out_sems.at[part])
        write.start()
        writes.append(write)
    for write in writes:
        write.wait()


def pack(queries, keys, values, rates_t):
    rows, width = queries.shape
    heads = width // HDIM
    return pl.pallas_call(
        pack_body,
        in_specs=[pl.BlockSpec(memory_space=pl.ANY)] * 4,
        out_specs=pl.BlockSpec(memory_space=pl.ANY),
        out_shape=jax.ShapeDtypeStruct((heads, rows + 24, LANES), bf16),
        scratch_shapes=[
            pltpu.VMEM((rows, width), bf16),
            pltpu.VMEM((rows, width), bf16),
            pltpu.VMEM((rows, width), bf16),
            pltpu.VMEM((heads, rows), bf16),
            pltpu.VMEM((heads, rows + 24, LANES), bf16),
            pltpu.VMEM((heads, LANES), f32),
            pltpu.SemaphoreType.DMA((PACK_PARTS, 4)),
            pltpu.SemaphoreType.DMA((PACK_PARTS,)),
        ],
        compiler_params=pltpu.CompilerParams(vmem_limit_bytes=PACK_LIMIT),
        name="pack",
    )(queries, keys, values, rates_t)


def packed(x):
    hi, lo = split(x)
    return jnp.where(lanes_left(x.shape[0]), hi.astype(f32), lo.astype(f32)).astype(bf16)


def twice(p):
    return jnp.concatenate([p, p], axis=1)


def four(hi, lo):
    return jnp.concatenate([hi, hi, lo, lo], axis=0)


def doubled_eye():
    row = lax.broadcasted_iota(jnp.int32, (HDIM, LANES), 0)
    col = lax.broadcasted_iota(jnp.int32, (HDIM, LANES), 1)
    return jnp.where(row == lax.rem(col, HDIM), 1.0, 0.0).astype(f32)


def norm_sums():
    row = lax.broadcasted_iota(jnp.int32, (2 * LANES, 2 * LANES), 0)
    col = lax.broadcasted_iota(jnp.int32, (2 * LANES, 2 * LANES), 1)
    is_key_row = lax.rem(row, LANES) >= HDIM
    return jnp.where(is_key_row == (col < LANES), 1.0, 0.0).astype(bf16)


def inverse_norms(qk, sums):
    hi, lo = split(qk * qk)
    return lax.rsqrt(mm(jnp.concatenate([hi, lo], axis=1), sums) + 1e-06)


def attend_body(
    tv_ref, me_ref, recv_ref, msg_ref, qk_ref, ar_ref, g_ref,
    qk_scr, v_scr, r_scr, inv_scr, rate_scr, k2_scr, qs_scr, tf_scr, tb_scr, da_scr, ckh_scr, ckl_scr, h_scr, reach_scr,
):
    groups, rows, _ = recv_ref.shape
    toks = rows - 24
    late = toks - 24
    seglen = groups * toks
    chunks = seglen // GROUP
    blocks = seglen // QROWS
    valid = tv_ref[0]
    me = me_ref[0]

    pick = lax.broadcasted_iota(jnp.int32, (toks, LANES), 0) == lax.broadcasted_iota(jnp.int32, (toks, LANES), 1)
    left24, left_late = lanes_left(24), lanes_left(late)
    for g in range(groups):
        block = recv_ref[g].astype(f32)
        base = toks * g
        qk_scr[base : base + toks] = block[0:toks]
        tail = block[toks : toks + 24]
        tail_sw = swap_halves(tail)
        v_scr[base : base + 24] = jnp.where(left24, tail_sw, tail)
        v_scr[base + 24 : base + toks] = jnp.where(left_late, tail[0:late], tail_sw[0:late])
        r_scr[base : base + toks] = jnp.where(pick, tail[late : late + 1], 0.0)

    sums = norm_sums()
    ones = jnp.ones((LANES, LANES), bf16)
    left = lanes_left(QROWS)

    for b in range(blocks):
        at = slice(QROWS * b, QROWS * (b + 1))
        inv_scr[at] = inverse_norms(qk_scr[at], sums)[:, 0:LANES]
        rate = mm(r_scr[at].astype(bf16), ones)
        if QROWS * b < TEXT:
            position = QROWS * b + lax.broadcasted_iota(jnp.int32, (QROWS, LANES), 0)
            rate = jnp.where((position >= TEXT) | (position < valid), rate, 0.0)
        rate_scr[at] = rate
    for b in range(blocks):
        at = slice(QROWS * b, QROWS * (b + 1))
        qk = qk_scr[at]
        kq = swap_halves(qk)
        k2 = jnp.where(left, kq, qk)
        k2_scr[at] = k2.astype(bf16)
        qk_ref[at] = qk.astype(bf16)
        qs_scr[at] = jnp.where(left, qk * (1.0 / math.sqrt(HDIM)), 0.0).astype(bf16)
        inv_k = inv_scr[at]
        step = rate_scr[at] * inv_k
        inv_scr[at] = step
        ck_hi, ck_lo = split(step * inv_k * k2)
        ckh_scr[at] = ck_hi
        ckl_scr[at] = ck_lo
    for n in range(chunks):
        at = slice(GROUP * n, GROUP * (n + 1))
        k = k2_scr[at, 0:HDIM]
        gram = mm_tn(jnp.concatenate([k, k], axis=0), jnp.concatenate([ckh_scr[at], ckl_scr[at]], axis=0))
        g_hi, g_lo = split(gram)
        g_ref[n, 0:HDIM] = g_hi
        g_ref[n, HDIM : 2 * HDIM] = g_lo

    v2 = v_scr[...].astype(bf16)
    eye = doubled_eye()
    t_f, t_b = eye, eye

    def gram_right(n):
        return four(g_ref[n, 0:HDIM], g_ref[n, HDIM : 2 * HDIM])

    for m in range(chunks // 2):
        g0, g1 = (g_ref[2 * m + i, 0:HDIM].astype(f32) + g_ref[2 * m + i, HDIM : 2 * HDIM].astype(f32) for i in (0, 1))
        pair = g0 + g1 - mm(twice(packed(g0)), gram_right(2 * m + 1))
        hi, lo = split(pair)
        h_scr[m, 0:HDIM] = hi
        h_scr[m, HDIM : 2 * HDIM] = lo

    def advance_f(t, m):
        p = packed(t)
        keep(tf_scr, 2 * m, p)
        keep(tf_scr, 2 * m + 1, packed(t - mm(twice(p), gram_right(2 * m))))
        return t - mm(twice(p), four(h_scr[m, 0:HDIM], h_scr[m, HDIM : 2 * HDIM]))

    def advance_b(t, m):
        p = packed(t)
        keep(tb_scr, 2 * m + 1, p)
        keep(tb_scr, 2 * m, packed(t - mm(twice(p), gram_right(2 * m + 1))))
        hi, lo = h_scr[m, 0:HDIM], h_scr[m, HDIM : 2 * HDIM]
        row = jnp.concatenate([hi, lo], axis=1)
        return t - mm_nt(twice(p), jnp.concatenate([row, row], axis=0))

    def keep(ref, n, p):
        ref[GROUP * n : GROUP * (n + 1)] = p

    parts = seglen // AROWS
    cols = lax.broadcasted_iota(jnp.int32, (AROWS, TEXT), 1)
    left_part = lanes_left(AROWS)

    def scores_of(b):
        scores = mm_nt(qs_scr[AROWS * b : AROWS * (b + 1)], k2_scr[...])
        return jnp.concatenate([jnp.where(cols < valid, scores[:, 0:TEXT], -1e30), scores[:, TEXT:]], axis=1)

    def close(b, raised, row_total):
        at = slice(AROWS * b, AROWS * (b + 1))
        att = (mm(raised, v2) / row_total).astype(bf16).astype(f32)
        ar_ref[at] = jnp.where(left_part, att, rate_scr[at]).astype(bf16)
        da_scr[at] = packed(inv_scr[at] * att)

    scores = scores_of(0)
    for b in range(parts):
        if b:
            close(b - 1, raised, row_total)
        following = scores_of(b + 1) if b + 1 < parts else None
        for m in range(chunks // 2 * b // parts, chunks // 2 * (b + 1) // parts):
            t_f = advance_f(t_f, m)
            t_b = advance_b(t_b, chunks // 2 - 1 - m)
        peak = jnp.max(scores, axis=1, keepdims=True)
        raised = jnp.exp(scores - peak)
        row_total = jnp.sum(raised, axis=1, keepdims=True)
        raised = raised.astype(bf16)
        scores = following
    close(parts - 1, raised, row_total)

    for n in range(chunks):
        at = slice(GROUP * n, GROUP * (n + 1))
        hi, lo = split(mm_nt(k2_scr[at], jnp.concatenate([tf_scr[at], tb_scr[at]], axis=0)))
        reach_scr[at] = jnp.concatenate([hi, lo], axis=1)
    total = mm_tn(da_scr[...], reach_scr[...])
    total = total[0:HDIM] + total[HDIM : 2 * HDIM]
    shift_f = total[:, 0:LANES] + total[:, LANES : 2 * LANES]
    shift_b = swap_halves(shift_f)
    left64 = lanes_left(HDIM)
    later = jnp.where(left64, t_f - eye, shift_f)
    earlier = jnp.where(left64, t_b - eye, shift_b)
    for s in range(msg_ref.shape[0]):
        msg_ref[s] = jnp.where(s > me, later, earlier).astype(msg_ref.dtype)


def attend(text_valid, me, received, segments, link):
    groups, rows, _ = received.shape
    seglen = groups * (rows - 24)
    chunks = seglen // GROUP
    smem = pl.BlockSpec(memory_space=pltpu.SMEM)
    vmem = pl.BlockSpec(memory_space=pltpu.VMEM)
    tall = (seglen, LANES)
    return pl.pallas_call(
        attend_body,
        in_specs=[smem, smem, vmem],
        out_specs=[vmem] * 4,
        out_shape=[jax.ShapeDtypeStruct((segments, HDIM, LANES), link)]
        + [jax.ShapeDtypeStruct(tall, bf16)] * 2
        + [jax.ShapeDtypeStruct((chunks, LANES, LANES), bf16)],
        scratch_shapes=[
            *[pltpu.VMEM(tall, f32)] * 5, *[pltpu.VMEM(tall, bf16)] * 7, pltpu.VMEM((chunks // 2, LANES, LANES), bf16),
            pltpu.VMEM((seglen, 2 * LANES), bf16),
        ],
        compiler_params=pltpu.CompilerParams(vmem_limit_bytes=VMEM_LIMIT),
        name="attend",
    )(text_valid, me, received)


def operators_body(
    qk_ref, ar_ref, g_ref, base_ref, ehi_ref, elo_ref,
    opf_scr, opb_scr, xf_scr, xb_scr, shift_scr, yhi_scr, ylo_scr, k2_scr, q2_scr, inv_scr,
):
    chunks = g_ref.shape[0]
    row_id = lax.broadcasted_iota(jnp.int32, (GROUP, LANES), 0)
    col_id = lax.rem(lax.broadcasted_iota(jnp.int32, (GROUP, LANES), 1), GROUP)
    left = lanes_left(GROUP)
    sums = norm_sums()
    eye = doubled_eye()
    x_f = jnp.concatenate([eye, jnp.zeros_like(eye)], axis=0)
    x_b = x_f

    def rows_of(n):
        return slice(GROUP * n, GROUP * (n + 1))

    def halves(x):
        x = x.astype(f32)
        x_sw = swap_halves(x)
        on_left = lanes_left(x.shape[0])
        return jnp.where(on_left, x, x_sw), jnp.where(on_left, x_sw, x)

    def advance(x, n, keep_ref):
        hi, lo = split(x)
        keep_ref[n] = jnp.concatenate([hi, lo], axis=1)
        p = jnp.where(lanes_left(2 * HDIM), hi.astype(f32), lo.astype(f32)).astype(bf16)
        x = x - mm(twice(p), four(g_ref[n, 0:HDIM], g_ref[n, HDIM : 2 * HDIM]))
        return jnp.concatenate([x[0:HDIM], x[HDIM : 2 * HDIM] + shift_scr[n]], axis=0)

    blocks = chunks * GROUP // QROWS
    for b in range(blocks):
        at = slice(QROWS * b, QROWS * (b + 1))
        inv_scr[at] = inverse_norms(qk_ref[at].astype(f32), sums)
    for b in range(blocks):
        at = slice(QROWS * b, QROWS * (b + 1))
        inv_k = inv_scr[at, 0:LANES]
        q2, k2 = halves(qk_ref[at])
        att, rate = halves(ar_ref[at])
        step = rate * inv_k
        ck_hi, ck_lo = split(step * inv_k * k2)
        da_hi, da_lo = split(step * att)
        yhi_scr[at] = jnp.concatenate([ck_hi, da_hi], axis=1)
        ylo_scr[at] = jnp.concatenate([ck_lo, da_lo], axis=1)
        base_ref[at] = att
        q2_scr[at] = q2.astype(bf16)
        k2_scr[at] = k2.astype(bf16)
    for n in range(chunks):
        at = rows_of(n)
        k2 = k2_scr[at]
        da = jnp.concatenate([yhi_scr[at, LANES : LANES + HDIM], ylo_scr[at, LANES : LANES + HDIM]], axis=0)
        shift_scr[n] = mm_tn(da, jnp.concatenate([k2, k2], axis=0))

    for n in range(chunks):
        x_f = advance(x_f, n, xf_scr)
        x_b = advance(x_b, chunks - 1 - n, xb_scr)
        at = rows_of(n)
        q2, k2 = q2_scr[at].astype(f32), k2_scr[at]
        scores = mm_nt(jnp.where(left, q2, 0.0).astype(bf16), jnp.concatenate([k2, k2], axis=0))
        both = packed(
            jnp.concatenate(
                [jnp.where(col_id <= row_id, scores, 0.0), jnp.where(col_id >= row_id, scores, 0.0)], axis=0
            )
        )
        y_hi, y_lo = yhi_scr[at], ylo_scr[at]
        pushed = mm(twice(both), four(y_hi, y_lo))
        scale = math.sqrt(HDIM) * inv_scr[at, LANES : 2 * LANES]
        opf_scr[at] = packed(scale * (q2 - pushed[0:GROUP, 0:LANES]))
        opb_scr[at] = packed(scale * (q2 - pushed[GROUP : 2 * GROUP, 0:LANES]))
        base_ref[at] = base_ref[at] + scale * (
            pushed[0:GROUP, LANES : 2 * LANES] + pushed[GROUP : 2 * GROUP, LANES : 2 * LANES]
        )

    for n in range(chunks):
        at = rows_of(n)

        def through(op_ref, x_ref):
            t, w = x_ref[n, 0:HDIM], x_ref[n, HDIM : 2 * HDIM]
            return mm_nt(twice(op_ref[at]), jnp.concatenate([t, t, w, w], axis=0))

        from_f, from_b = through(opf_scr, xf_scr), through(opb_scr, xb_scr)
        base_ref[at] = base_ref[at] + from_f[:, LANES : 2 * LANES] + from_b[:, LANES : 2 * LANES]
        e_hi, e_lo = split(jnp.where(left, from_f[:, 0:LANES], from_b[:, 0:LANES]))
        ehi_ref[at] = e_hi
        elo_ref[at] = e_lo


def operators(*held):
    tall = held[0].shape
    chunks = tall[0] // GROUP
    state = (chunks, 2 * HDIM, 2 * LANES)
    return pl.pallas_call(
        operators_body,
        out_shape=[
            jax.ShapeDtypeStruct(tall, f32),
            jax.ShapeDtypeStruct(tall, bf16),
            jax.ShapeDtypeStruct(tall, bf16),
        ],
        scratch_shapes=[
            pltpu.VMEM(tall, bf16), pltpu.VMEM(tall, bf16), pltpu.VMEM(state, bf16), pltpu.VMEM(state, bf16),
            pltpu.VMEM((chunks, HDIM, LANES), f32),
            pltpu.VMEM((tall[0], 2 * LANES), bf16), pltpu.VMEM((tall[0], 2 * LANES), bf16),
            pltpu.VMEM(tall, bf16), pltpu.VMEM(tall, bf16), pltpu.VMEM((tall[0], 2 * LANES), f32),
        ],
        compiler_params=pltpu.CompilerParams(vmem_limit_bytes=VMEM_LIMIT),
        cost_estimate=pl.CostEstimate(flops=2_000_000_000, bytes_accessed=8_000_000, transcendentals=0),
        name="operators",
    )(*held)


def finish_body(me_ref, msg_ref, sf_ref, sb_ref, base_ref, ehi_ref, elo_ref, out_ref):
    segments = msg_ref.shape[0]
    groups, quad, wide = out_ref.shape
    half = quad * wide // LANES
    me = me_ref[0]
    left64 = lanes_left(HDIM)

    def doubled_transpose(state):
        return jnp.concatenate([state, state], axis=0).T

    def times(x, decay):
        return mm(twice(packed(x)), four(*split(decay)))

    def times_sent(x, decay):
        decay = decay.astype(bf16)
        return mm(packed(x), jnp.concatenate([decay, decay], axis=0))

    def leaf(i):
        m = msg_ref[i].astype(f32)
        m_sw = swap_halves(m)
        return jnp.concatenate([jnp.where(left64, m, m_sw), jnp.where(left64, m_sw, m)], axis=0)

    def then(first, second, times):
        return first + second + times(first, second[0:HDIM])

    def sibling(level):
        size = 2**level
        block = lax.div(me, size)
        before = lax.rem(block, 2) == 1
        start = jnp.where(before, block - 1, block + 1) * size
        nodes = [leaf(start + jnp.where(before, i, size - 1 - i)) for i in range(size)]
        way = times_sent
        while len(nodes) > 1:
            nodes = [then(nodes[i], nodes[i + 1], way) for i in range(0, len(nodes), 2)]
            way = times
        return before, nodes[0], way

    w_f, w_b = doubled_transpose(sf_ref[0]), doubled_transpose(sb_ref[0])
    for before, node, way in [sibling(level) for level in reversed(range(segments.bit_length() - 1))]:
        state = jnp.where(before, w_f, w_b)
        state = state + way(state, node[0:HDIM]) + node[HDIM : 2 * HDIM]
        w_f, w_b = jnp.where(before, state, w_f), jnp.where(before, w_b, state)
    w_hi, w_lo = split(jnp.where(left64, w_f, w_b))
    w_row = jnp.concatenate([w_hi, w_hi, w_lo], axis=1)
    e_hi = ehi_ref[...]
    got = mm_nt(jnp.concatenate([e_hi, elo_ref[...], e_hi], axis=1), jnp.concatenate([w_row, w_row], axis=0))
    whole = got + base_ref[...]
    left = lanes_left(2 * quad)
    for g in range(groups):
        for j in range(wide // LANES):
            row = 2 * half * g + 2 * quad * j
            rows = whole[row : row + 2 * quad]
            both = jnp.where(left, rows, pltpu.roll(rows, quad, 0))
            out_ref[g, :, LANES * j : LANES * (j + 1)] = both[0:quad].astype(bf16)


def finish(me, maps, state_fwd, state_bwd, base, ehi, elo, groups):
    seglen = base.shape[0]
    half = seglen // groups // 2
    smem = pl.BlockSpec(memory_space=pltpu.SMEM)
    vmem = pl.BlockSpec(memory_space=pltpu.VMEM)
    return pl.pallas_call(
        finish_body,
        in_specs=[smem] + [vmem] * 6,
        out_specs=vmem,
        out_shape=jax.ShapeDtypeStruct((groups, QUAD, half // QUAD * LANES), bf16),
        compiler_params=pltpu.CompilerParams(vmem_limit_bytes=VMEM_LIMIT),
        name="finish",
    )(me, maps, state_fwd, state_bwd, base, ehi, elo)


def unpack_body(x_ref, out_ref, scr, rows_scr):
    heads, quad, wide = x_ref.shape
    half = quad * wide // LANES
    left = lanes_left(half)
    for head in range(heads):
        for j in range(wide // LANES):
            rows_scr[head, quad * j : quad * (j + 1)] = x_ref[head, :, LANES * j : LANES * (j + 1)].astype(f32)
    for p in range(heads // 2):
        even = rows_scr[2 * p]
        odd = rows_scr[2 * p + 1]
        first = jnp.where(left, even, swap_halves(odd))
        second = jnp.where(left, swap_halves(even), odd)
        for j in range(wide // LANES):
            scr[p, 2 * quad * j : 2 * quad * j + quad] = first[quad * j : quad * (j + 1)]
            scr[p, 2 * quad * j + quad : 2 * quad * (j + 1)] = second[quad * j : quad * (j + 1)]
    for p in range(heads // 2):
        out_ref[:, LANES * p : LANES * (p + 1)] = scr[p].astype(bf16)


def unpack(x):
    heads, quad, wide = x.shape
    half = quad * wide // LANES
    return pl.pallas_call(
        unpack_body,
        out_shape=jax.ShapeDtypeStruct((2 * half, heads * HDIM), bf16),
        scratch_shapes=[pltpu.VMEM((heads // 2, 2 * half, LANES), f32), pltpu.VMEM((heads, half, LANES), f32)],
        compiler_params=pltpu.CompilerParams(vmem_limit_bytes=VMEM_LIMIT),
        name="unpack",
    )(x)


def exchange(x, axis):
    return lax.all_to_all(x, axis, split_axis=0, concat_axis=0, tiled=True)


def local(queries, keys, values, rates, text_valid, state_fwd, state_bwd):
    segments = lax.axis_size("seg")
    groups = lax.axis_size("grp")
    me = lax.axis_index("seg").astype(jnp.int32).reshape(1)
    received = exchange(pack(queries, keys, values, rates.T), "grp")
    msg, *held = attend(text_valid, me, received, segments, bf16)
    maps = exchange(msg, "seg")
    base, ehi, elo = operators(*held)
    mixed = finish(me, maps, state_fwd, state_bwd, base, ehi, elo, groups)
    return unpack(exchange(mixed, "grp"))


def solution(mesh):
    in_specs = (
        P(("seg", "grp"), None),
        P(("seg", "grp"), None),
        P(("seg", "grp"), None),
        P(("seg", "grp"), None),
        P("seg"),
        P("grp", None, None),
        P("grp", None, None),
    )
    out_specs = P(("seg", "grp"), None)
    return jax.shard_map(local, mesh=mesh, in_specs=in_specs, out_specs=out_specs, check_vma=False)
```

```python
import math

import jax
import jax.numpy as jnp
from jax import lax
from jax.experimental import pallas as pl
from jax.experimental.pallas import tpu as pltpu
from jax.sharding import PartitionSpec as P

GROUP = 64
TEXT = 128
HDIM = 64
LANES = 128
QROWS = 256
AROWS = 128
QUAD = 4
PACK_PARTS = 2
VMEM_LIMIT = 24 * 1024 * 1024
PACK_LIMIT = 62 * 1024 * 1024

bf16 = jnp.bfloat16
f32 = jnp.float32


def split(x):
    hi = x.astype(bf16)
    return hi, (x - hi.astype(f32)).astype(bf16)


def mm(a, b):
    return lax.dot_general(a, b, (((1,), (0,)), ((), ())), preferred_element_type=f32)


def mm_nt(a, b):
    return lax.dot_general(a, b, (((1,), (1,)), ((), ())), preferred_element_type=f32)


def mm_tn(a, b):
    return lax.dot_general(a, b, (((0,), (0,)), ((), ())), preferred_element_type=f32)


def lanes_left(rows):
    return lax.broadcasted_iota(jnp.int32, (rows, LANES), 1) < HDIM


def swap_halves(x):
    return pltpu.roll(x, HDIM, 1)


def pack_body(q_hbm, k_hbm, v_hbm, r_hbm, o_hbm, q_ref, k_ref, v_ref, r_ref, o_ref, rate_scr, in_sems, out_sems):
    rows, width = q_ref.shape
    heads = width // HDIM
    late = rows - 24
    parts = in_sems.shape[0]
    wide = width // parts
    each = heads // parts
    rate_copy = pltpu.make_async_copy(r_hbm, r_ref, in_sems.at[0, 3])
    rate_copy.start()
    reads, writes = [], []
    for part in range(parts):
        cols = pl.ds(wide * part, wide)
        reads.append(
            [
                pltpu.make_async_copy(source.at[:, cols], target.at[:, cols], in_sems.at[part, i])
                for i, (source, target) in enumerate(((q_hbm, q_ref), (k_hbm, k_ref), (v_hbm, v_ref)))
            ]
        )
        for read in reads[part]:
            read.start()
    left = lanes_left(rows)
    left24 = lanes_left(24)
    rate_scr[...] = jnp.zeros_like(rate_scr)
    rate_copy.wait()
    rate_scr[:, 0:rows] = r_ref[...].astype(f32)
    for part in range(parts):
        for read in reads[part]:
            read.wait()
        for p in range(each // 2 * part, each // 2 * (part + 1)):
            cols = slice(LANES * p, LANES * (p + 1))
            q = q_ref[:, cols].astype(f32)
            k = k_ref[:, cols].astype(f32)
            v = v_ref[:, cols].astype(f32)
            q_sw, k_sw, v_sw = swap_halves(q), swap_halves(k), swap_halves(v)
            for odd in (0, 1):
                head = 2 * p + odd
                qk = jnp.where(left, q_sw, k) if odd else jnp.where(left, q, k_sw)
                v_right, v_left = (v, v_sw) if odd else (v_sw, v)
                rate = jnp.broadcast_to(rate_scr[head : head + 1, :], (24 - late, LANES))
                low = jnp.concatenate([v_left[24:rows], rate], axis=0)
                vr = jnp.where(left24, low, v_right[0:24])
                o_ref[head] = jnp.concatenate([qk, vr], axis=0).astype(bf16)
            if p % 4 == 3:
                own = pl.ds(2 * p - 6, 8)
                write = pltpu.make_async_copy(o_ref.at[own], o_hbm.at[own], out_sems.at[p // 4])
                write.start()
                writes.append(write)
    for write in writes:
        write.wait()


def pack(queries, keys, values, rates_t):
    rows, width = queries.shape
    heads = width // HDIM
    return pl.pallas_call(
        pack_body,
        in_specs=[pl.BlockSpec(memory_space=pl.ANY)] * 4,
        out_specs=pl.BlockSpec(memory_space=pl.ANY),
        out_shape=jax.ShapeDtypeStruct((heads, rows + 24, LANES), bf16),
        scratch_shapes=[
            pltpu.VMEM((rows, width), bf16),
            pltpu.VMEM((rows, width), bf16),
            pltpu.VMEM((rows, width), bf16),
            pltpu.VMEM((heads, rows), bf16),
            pltpu.VMEM((heads, rows + 24, LANES), bf16),
            pltpu.VMEM((heads, LANES), f32),
            pltpu.SemaphoreType.DMA((PACK_PARTS, 4)),
            pltpu.SemaphoreType.DMA((heads // 8,)),
        ],
        compiler_params=pltpu.CompilerParams(vmem_limit_bytes=PACK_LIMIT),
        name="pack",
    )(queries, keys, values, rates_t)


def packed(x):
    hi, lo = split(x)
    return jnp.where(lanes_left(x.shape[0]), hi.astype(f32), lo.astype(f32)).astype(bf16)


def twice(p):
    return jnp.concatenate([p, p], axis=1)


def four(hi, lo):
    return jnp.concatenate([hi, hi, lo, lo], axis=0)


def doubled_eye():
    row = lax.broadcasted_iota(jnp.int32, (HDIM, LANES), 0)
    col = lax.broadcasted_iota(jnp.int32, (HDIM, LANES), 1)
    return jnp.where(row == lax.rem(col, HDIM), 1.0, 0.0).astype(f32)


def norm_sums():
    row = lax.broadcasted_iota(jnp.int32, (2 * LANES, 2 * LANES), 0)
    col = lax.broadcasted_iota(jnp.int32, (2 * LANES, 2 * LANES), 1)
    is_key_row = lax.rem(row, LANES) >= HDIM
    return jnp.where(is_key_row == (col < LANES), 1.0, 0.0).astype(bf16)


def inverse_norms(qk, sums):
    hi, lo = split(qk * qk)
    return lax.rsqrt(mm(jnp.concatenate([hi, lo], axis=1), sums) + 1e-06)


def attend_body(
    tv_ref, me_ref, recv_ref, msg_ref, qk_ref, ar_ref, g_ref,
    qk_scr, v_scr, r_scr, inv_scr, rate_scr, k2_scr, qs_scr, tf_scr, tb_scr, da_scr, ckh_scr, ckl_scr, h_scr, reach_scr,
):
    groups, rows, _ = recv_ref.shape
    toks = rows - 24
    late = toks - 24
    seglen = groups * toks
    chunks = seglen // GROUP
    blocks = seglen // QROWS
    valid = tv_ref[0]
    me = me_ref[0]

    pick = lax.broadcasted_iota(jnp.int32, (toks, LANES), 0) == lax.broadcasted_iota(jnp.int32, (toks, LANES), 1)
    left24, left_late = lanes_left(24), lanes_left(late)
    for g in range(groups):
        block = recv_ref[g].astype(f32)
        base = toks * g
        qk_scr[base : base + toks] = block[0:toks]
        tail = block[toks : toks + 24]
        tail_sw = swap_halves(tail)
        v_scr[base : base + 24] = jnp.where(left24, tail_sw, tail)
        v_scr[base + 24 : base + toks] = jnp.where(left_late, tail[0:late], tail_sw[0:late])
        r_scr[base : base + toks] = jnp.where(pick, tail[late : late + 1], 0.0)

    sums = norm_sums()
    ones = jnp.ones((LANES, LANES), bf16)
    left = lanes_left(QROWS)

    for b in range(blocks):
        at = slice(QROWS * b, QROWS * (b + 1))
        inv_scr[at] = inverse_norms(qk_scr[at], sums)[:, 0:LANES]
        rate = mm(r_scr[at].astype(bf16), ones)
        if QROWS * b < TEXT:
            position = QROWS * b + lax.broadcasted_iota(jnp.int32, (QROWS, LANES), 0)
            rate = jnp.where((position >= TEXT) | (position < valid), rate, 0.0)
        rate_scr[at] = rate
    for b in range(blocks):
        at = slice(QROWS * b, QROWS * (b + 1))
        qk = qk_scr[at]
        kq = swap_halves(qk)
        k2 = jnp.where(left, kq, qk)
        k2_scr[at] = k2.astype(bf16)
        qk_ref[at] = qk.astype(bf16)
        qs_scr[at] = jnp.where(left, qk * (1.0 / math.sqrt(HDIM)), 0.0).astype(bf16)
        inv_k = inv_scr[at]
        step = rate_scr[at] * inv_k
        inv_scr[at] = step
        ck_hi, ck_lo = split(step * inv_k * k2)
        ckh_scr[at] = ck_hi
        ckl_scr[at] = ck_lo
    for n in range(chunks):
        at = slice(GROUP * n, GROUP * (n + 1))
        k = k2_scr[at, 0:HDIM]
        gram = mm_tn(jnp.concatenate([k, k], axis=0), jnp.concatenate([ckh_scr[at], ckl_scr[at]], axis=0))
        g_hi, g_lo = split(gram)
        g_ref[n, 0:HDIM] = g_hi
        g_ref[n, HDIM : 2 * HDIM] = g_lo

    v2 = v_scr[...].astype(bf16)
    eye = doubled_eye()
    t_f, t_b = eye, eye

    def gram_right(n):
        return four(g_ref[n, 0:HDIM], g_ref[n, HDIM : 2 * HDIM])

    for m in range(chunks // 2):
        g0, g1 = (g_ref[2 * m + i, 0:HDIM].astype(f32) + g_ref[2 * m + i, HDIM : 2 * HDIM].astype(f32) for i in (0, 1))
        pair = g0 + g1 - mm(twice(packed(g0)), gram_right(2 * m + 1))
        hi, lo = split(pair)
        h_scr[m, 0:HDIM] = hi
        h_scr[m, HDIM : 2 * HDIM] = lo

    def advance_f(t, m):
        p = packed(t)
        keep(tf_scr, 2 * m, p)
        keep(tf_scr, 2 * m + 1, packed(t - mm(twice(p), gram_right(2 * m))))
        return t - mm(twice(p), four(h_scr[m, 0:HDIM], h_scr[m, HDIM : 2 * HDIM]))

    def advance_b(t, m):
        p = packed(t)
        keep(tb_scr, 2 * m + 1, p)
        keep(tb_scr, 2 * m, packed(t - mm(twice(p), gram_right(2 * m + 1))))
        hi, lo = h_scr[m, 0:HDIM], h_scr[m, HDIM : 2 * HDIM]
        row = jnp.concatenate([hi, lo], axis=1)
        return t - mm_nt(twice(p), jnp.concatenate([row, row], axis=0))

    def keep(ref, n, p):
        ref[GROUP * n : GROUP * (n + 1)] = p

    parts = seglen // AROWS
    cols = lax.broadcasted_iota(jnp.int32, (AROWS, TEXT), 1)
    left_part = lanes_left(AROWS)

    def scores_of(b):
        scores = mm_nt(qs_scr[AROWS * b : AROWS * (b + 1)], k2_scr[...])
        return jnp.concatenate([jnp.where(cols < valid, scores[:, 0:TEXT], -1e30), scores[:, TEXT:]], axis=1)

    def close(b, raised, row_total):
        at = slice(AROWS * b, AROWS * (b + 1))
        att = (mm(raised, v2) / row_total).astype(bf16).astype(f32)
        ar_ref[at] = jnp.where(left_part, att, rate_scr[at]).astype(bf16)
        da_scr[at] = packed(inv_scr[at] * att)

    def reach(n):
        at = slice(GROUP * n, GROUP * (n + 1))
        hi, lo = split(mm_nt(k2_scr[at], jnp.concatenate([tf_scr[at], tb_scr[at]], axis=0)))
        reach_scr[at] = jnp.concatenate([hi, lo], axis=1)

    scores = scores_of(0)
    for m in range(2):
        t_f = advance_f(t_f, m)
        t_b = advance_b(t_b, chunks // 2 - 1 - m)
    for b in range(parts):
        if b:
            close(b - 1, raised, row_total)
        following = scores_of(b + 1) if b + 1 < parts else None
        if b + 2 < chunks // 2:
            t_f = advance_f(t_f, b + 2)
            t_b = advance_b(t_b, chunks // 2 - 1 - b - 2)
        else:
            own = 10 * (b + 2 - chunks // 2)
            for n in range(own, own + 10):
                reach(n)
        peak = jnp.max(scores, axis=1, keepdims=True)
        raised = jnp.exp(scores - peak)
        row_total = jnp.sum(raised, axis=1, keepdims=True)
        raised = raised.astype(bf16)
        scores = following
    close(parts - 1, raised, row_total)

    total = mm_tn(da_scr[...], reach_scr[...])
    total = total[0:HDIM] + total[HDIM : 2 * HDIM]
    shift_f = total[:, 0:LANES] + total[:, LANES : 2 * LANES]
    shift_b = swap_halves(shift_f)
    left64 = lanes_left(HDIM)
    later = jnp.where(left64, t_f - eye, shift_f)
    earlier = jnp.where(left64, t_b - eye, shift_b)
    for s in range(msg_ref.shape[0]):
        msg_ref[s] = jnp.where(s > me, later, earlier).astype(msg_ref.dtype)


def attend(text_valid, me, received, segments, link):
    groups, rows, _ = received.shape
    seglen = groups * (rows - 24)
    chunks = seglen // GROUP
    smem = pl.BlockSpec(memory_space=pltpu.SMEM)
    vmem = pl.BlockSpec(memory_space=pltpu.VMEM)
    tall = (seglen, LANES)
    return pl.pallas_call(
        attend_body,
        in_specs=[smem, smem, vmem],
        out_specs=[vmem] * 4,
        out_shape=[jax.ShapeDtypeStruct((segments, HDIM, LANES), link)]
        + [jax.ShapeDtypeStruct(tall, bf16)] * 2
        + [jax.ShapeDtypeStruct((chunks, LANES, LANES), bf16)],
        scratch_shapes=[
            *[pltpu.VMEM(tall, f32)] * 5, *[pltpu.VMEM(tall, bf16)] * 7, pltpu.VMEM((chunks // 2, LANES, LANES), bf16),
            pltpu.VMEM((seglen, 2 * LANES), bf16),
        ],
        compiler_params=pltpu.CompilerParams(vmem_limit_bytes=VMEM_LIMIT),
        name="attend",
    )(text_valid, me, received)


def operators_body(
    qk_ref, ar_ref, g_ref, base_ref, ehi_ref, elo_ref,
    opf_scr, opb_scr, xf_scr, xb_scr, shift_scr, yhi_scr, ylo_scr, k2_scr, q2_scr, inv_scr,
):
    chunks = g_ref.shape[0]
    row_id = lax.broadcasted_iota(jnp.int32, (GROUP, LANES), 0)
    col_id = lax.rem(lax.broadcasted_iota(jnp.int32, (GROUP, LANES), 1), GROUP)
    left = lanes_left(GROUP)
    sums = norm_sums()
    eye = doubled_eye()
    x_f = jnp.concatenate([eye, jnp.zeros_like(eye)], axis=0)
    x_b = x_f

    def rows_of(n):
        return slice(GROUP * n, GROUP * (n + 1))

    def halves(x):
        x = x.astype(f32)
        x_sw = swap_halves(x)
        on_left = lanes_left(x.shape[0])
        return jnp.where(on_left, x, x_sw), jnp.where(on_left, x_sw, x)

    def advance(x, n, keep_ref):
        hi, lo = split(x)
        keep_ref[n] = jnp.concatenate([hi, lo], axis=1)
        p = jnp.where(lanes_left(2 * HDIM), hi.astype(f32), lo.astype(f32)).astype(bf16)
        x = x - mm(twice(p), four(g_ref[n, 0:HDIM], g_ref[n, HDIM : 2 * HDIM]))
        return jnp.concatenate([x[0:HDIM], x[HDIM : 2 * HDIM] + shift_scr[n]], axis=0)

    blocks = chunks * GROUP // QROWS
    for b in range(blocks):
        at = slice(QROWS * b, QROWS * (b + 1))
        inv_scr[at] = inverse_norms(qk_ref[at].astype(f32), sums)
    for b in range(blocks):
        at = slice(QROWS * b, QROWS * (b + 1))
        inv_k = inv_scr[at, 0:LANES]
        q2, k2 = halves(qk_ref[at])
        att, rate = halves(ar_ref[at])
        step = rate * inv_k
        ck_hi, ck_lo = split(step * inv_k * k2)
        da_hi, da_lo = split(step * att)
        yhi_scr[at] = jnp.concatenate([ck_hi, da_hi], axis=1)
        ylo_scr[at] = jnp.concatenate([ck_lo, da_lo], axis=1)
        base_ref[at] = att
        q2_scr[at] = q2.astype(bf16)
        k2_scr[at] = k2.astype(bf16)
    for n in range(chunks):
        at = rows_of(n)
        k2 = k2_scr[at]
        da = jnp.concatenate([yhi_scr[at, LANES : LANES + HDIM], ylo_scr[at, LANES : LANES + HDIM]], axis=0)
        shift_scr[n] = mm_tn(da, jnp.concatenate([k2, k2], axis=0))

    for n in range(chunks):
        x_f = advance(x_f, n, xf_scr)
        x_b = advance(x_b, chunks - 1 - n, xb_scr)
        at = rows_of(n)
        q2, k2 = q2_scr[at].astype(f32), k2_scr[at]
        scores = mm_nt(jnp.where(left, q2, 0.0).astype(bf16), jnp.concatenate([k2, k2], axis=0))
        both = packed(
            jnp.concatenate(
                [jnp.where(col_id <= row_id, scores, 0.0), jnp.where(col_id >= row_id, scores, 0.0)], axis=0
            )
        )
        y_hi, y_lo = yhi_scr[at], ylo_scr[at]
        pushed = mm(twice(both), four(y_hi, y_lo))
        scale = math.sqrt(HDIM) * inv_scr[at, LANES : 2 * LANES]
        opf_scr[at] = packed(scale * (q2 - pushed[0:GROUP, 0:LANES]))
        opb_scr[at] = packed(scale * (q2 - pushed[GROUP : 2 * GROUP, 0:LANES]))
        base_ref[at] = base_ref[at] + scale * (
            pushed[0:GROUP, LANES : 2 * LANES] + pushed[GROUP : 2 * GROUP, LANES : 2 * LANES]
        )

    for n in range(chunks):
        at = rows_of(n)

        def through(op_ref, x_ref):
            t, w = x_ref[n, 0:HDIM], x_ref[n, HDIM : 2 * HDIM]
            return mm_nt(twice(op_ref[at]), jnp.concatenate([t, t, w, w], axis=0))

        from_f, from_b = through(opf_scr, xf_scr), through(opb_scr, xb_scr)
        base_ref[at] = base_ref[at] + from_f[:, LANES : 2 * LANES] + from_b[:, LANES : 2 * LANES]
        e_hi, e_lo = split(jnp.where(left, from_f[:, 0:LANES], from_b[:, 0:LANES]))
        ehi_ref[at] = e_hi
        elo_ref[at] = e_lo


def operators(*held):
    tall = held[0].shape
    chunks = tall[0] // GROUP
    state = (chunks, 2 * HDIM, 2 * LANES)
    return pl.pallas_call(
        operators_body,
        out_shape=[
            jax.ShapeDtypeStruct(tall, f32),
            jax.ShapeDtypeStruct(tall, bf16),
            jax.ShapeDtypeStruct(tall, bf16),
        ],
        scratch_shapes=[
            pltpu.VMEM(tall, bf16), pltpu.VMEM(tall, bf16), pltpu.VMEM(state, bf16), pltpu.VMEM(state, bf16),
            pltpu.VMEM((chunks, HDIM, LANES), f32),
            pltpu.VMEM((tall[0], 2 * LANES), bf16), pltpu.VMEM((tall[0], 2 * LANES), bf16),
            pltpu.VMEM(tall, bf16), pltpu.VMEM(tall, bf16), pltpu.VMEM((tall[0], 2 * LANES), f32),
        ],
        compiler_params=pltpu.CompilerParams(vmem_limit_bytes=VMEM_LIMIT),
        cost_estimate=pl.CostEstimate(flops=2_000_000_000, bytes_accessed=8_000_000, transcendentals=0),
        name="operators",
    )(*held)


def finish_body(me_ref, msg_ref, sf_ref, sb_ref, base_ref, ehi_ref, elo_ref, out_ref):
    segments = msg_ref.shape[0]
    groups, quad, wide = out_ref.shape
    half = quad * wide // LANES
    me = me_ref[0]
    left64 = lanes_left(HDIM)

    def doubled_transpose(state):
        return jnp.concatenate([state, state], axis=0).T

    def times(x, decay):
        return mm(twice(packed(x)), four(*split(decay)))

    def times_sent(x, decay):
        decay = decay.astype(bf16)
        return mm(packed(x), jnp.concatenate([decay, decay], axis=0))

    def leaf(i):
        m = msg_ref[i].astype(f32)
        m_sw = swap_halves(m)
        return jnp.concatenate([jnp.where(left64, m, m_sw), jnp.where(left64, m_sw, m)], axis=0)

    def then(first, second, times):
        return first + second + times(first, second[0:HDIM])

    def sibling(level):
        size = 2**level
        block = lax.div(me, size)
        before = lax.rem(block, 2) == 1
        start = jnp.where(before, block - 1, block + 1) * size
        nodes = [leaf(start + jnp.where(before, i, size - 1 - i)) for i in range(size)]
        way = times_sent
        while len(nodes) > 1:
            nodes = [then(nodes[i], nodes[i + 1], way) for i in range(0, len(nodes), 2)]
            way = times
        return before, nodes[0], way

    w_f, w_b = doubled_transpose(sf_ref[0]), doubled_transpose(sb_ref[0])
    for before, node, way in [sibling(level) for level in reversed(range(segments.bit_length() - 1))]:
        state = jnp.where(before, w_f, w_b)
        state = state + way(state, node[0:HDIM]) + node[HDIM : 2 * HDIM]
        w_f, w_b = jnp.where(before, state, w_f), jnp.where(before, w_b, state)
    w_hi, w_lo = split(jnp.where(left64, w_f, w_b))
    w_row = jnp.concatenate([w_hi, w_hi, w_lo], axis=1)
    e_hi = ehi_ref[...]
    got = mm_nt(jnp.concatenate([e_hi, elo_ref[...], e_hi], axis=1), jnp.concatenate([w_row, w_row], axis=0))
    whole = got + base_ref[...]
    left = lanes_left(2 * quad)
    for g in range(groups):
        for j in range(wide // LANES):
            row = 2 * half * g + 2 * quad * j
            rows = whole[row : row + 2 * quad]
            both = jnp.where(left, rows, pltpu.roll(rows, quad, 0))
            out_ref[g, :, LANES * j : LANES * (j + 1)] = both[0:quad].astype(bf16)


def finish(me, maps, state_fwd, state_bwd, base, ehi, elo, groups):
    seglen = base.shape[0]
    half = seglen // groups // 2
    smem = pl.BlockSpec(memory_space=pltpu.SMEM)
    vmem = pl.BlockSpec(memory_space=pltpu.VMEM)
    return pl.pallas_call(
        finish_body,
        in_specs=[smem] + [vmem] * 6,
        out_specs=vmem,
        out_shape=jax.ShapeDtypeStruct((groups, QUAD, half // QUAD * LANES), bf16),
        compiler_params=pltpu.CompilerParams(vmem_limit_bytes=VMEM_LIMIT),
        name="finish",
    )(me, maps, state_fwd, state_bwd, base, ehi, elo)


def unpack_body(x_ref, out_ref, scr, rows_scr, out_scr, sems):
    heads, quad, wide = x_ref.shape
    half = quad * wide // LANES
    left = lanes_left(half)
    for head in range(heads):
        for j in range(wide // LANES):
            rows_scr[head, quad * j : quad * (j + 1)] = x_ref[head, :, LANES * j : LANES * (j + 1)].astype(f32)
    for p in range(heads // 2):
        even = rows_scr[2 * p]
        odd = rows_scr[2 * p + 1]
        first = jnp.where(left, even, swap_halves(odd))
        second = jnp.where(left, swap_halves(even), odd)
        for j in range(wide // LANES):
            scr[p, 2 * quad * j : 2 * quad * j + quad] = first[quad * j : quad * (j + 1)]
            scr[p, 2 * quad * j + quad : 2 * quad * (j + 1)] = second[quad * j : quad * (j + 1)]
    writes = []
    parts = sems.shape[0]
    each = heads // 2 // parts
    for part in range(parts):
        for p in range(each * part, each * (part + 1)):
            out_scr[:, LANES * p : LANES * (p + 1)] = scr[p].astype(bf16)
        cols = pl.ds(LANES * each * part, LANES * each)
        writes.append(pltpu.make_async_copy(out_scr.at[:, cols], out_ref.at[:, cols], sems.at[part]))
        writes[part].start()
    for write in writes:
        write.wait()


def unpack(x):
    heads, quad, wide = x.shape
    half = quad * wide // LANES
    return pl.pallas_call(
        unpack_body,
        out_specs=pl.BlockSpec(memory_space=pl.ANY),
        out_shape=jax.ShapeDtypeStruct((2 * half, heads * HDIM), bf16),
        scratch_shapes=[
            pltpu.VMEM((heads // 2, 2 * half, LANES), f32), pltpu.VMEM((heads, half, LANES), f32),
            pltpu.VMEM((2 * half, heads * HDIM), bf16), pltpu.SemaphoreType.DMA((2,)),
        ],
        compiler_params=pltpu.CompilerParams(vmem_limit_bytes=VMEM_LIMIT),
        name="unpack",
    )(x)


def exchange(x, axis):
    return lax.all_to_all(x, axis, split_axis=0, concat_axis=0, tiled=True)


def local(queries, keys, values, rates, text_valid, state_fwd, state_bwd):
    segments = lax.axis_size("seg")
    groups = lax.axis_size("grp")
    me = lax.axis_index("seg").astype(jnp.int32).reshape(1)
    received = exchange(pack(queries, keys, values, rates.T), "grp")
    msg, *held = attend(text_valid, me, received, segments, bf16)
    maps = exchange(msg, "seg")
    base, ehi, elo = operators(*held)
    mixed = finish(me, maps, state_fwd, state_bwd, base, ehi, elo, groups)
    return unpack(exchange(mixed, "grp"))


def solution(mesh):
    in_specs = (
        P(("seg", "grp"), None),
        P(("seg", "grp"), None),
        P(("seg", "grp"), None),
        P(("seg", "grp"), None),
        P("seg"),
        P("grp", None, None),
        P("grp", None, None),
    )
    out_specs = P(("seg", "grp"), None)
    return jax.shard_map(local, mesh=mesh, in_specs=in_specs, out_specs=out_specs, check_vma=False)
```

```python
import math

import jax
import jax.numpy as jnp
from jax import lax
from jax.experimental import pallas as pl
from jax.experimental.pallas import tpu as pltpu
from jax.sharding import PartitionSpec as P

GROUP = 64
TEXT = 128
HDIM = 64
LANES = 128
QROWS = 256
AROWS = 128
QUAD = 4
PACK_PARTS = 2
VMEM_LIMIT = 24 * 1024 * 1024
PACK_LIMIT = 62 * 1024 * 1024

bf16 = jnp.bfloat16
f32 = jnp.float32


def split(x):
    hi = x.astype(bf16)
    return hi, (x - hi.astype(f32)).astype(bf16)


def mm(a, b):
    return lax.dot_general(a, b, (((1,), (0,)), ((), ())), preferred_element_type=f32)


def mm_nt(a, b):
    return lax.dot_general(a, b, (((1,), (1,)), ((), ())), preferred_element_type=f32)


def mm_tn(a, b):
    return lax.dot_general(a, b, (((0,), (0,)), ((), ())), preferred_element_type=f32)


def lanes_left(rows):
    return lax.broadcasted_iota(jnp.int32, (rows, LANES), 1) < HDIM


def swap_halves(x):
    return pltpu.roll(x, HDIM, 1)


def pack_body(q_hbm, k_hbm, v_hbm, r_hbm, o_hbm, q_ref, k_ref, v_ref, r_ref, o_ref, rate_scr, in_sems, out_sems):
    rows, width = q_ref.shape
    heads = width // HDIM
    late = rows - 24
    parts = in_sems.shape[0]
    wide = width // parts
    each = heads // parts
    rate_copy = pltpu.make_async_copy(r_hbm, r_ref, in_sems.at[0, 3])
    rate_copy.start()
    reads, writes = [], []
    for part in range(parts):
        cols = pl.ds(wide * part, wide)
        reads.append(
            [
                pltpu.make_async_copy(source.at[:, cols], target.at[:, cols], in_sems.at[part, i])
                for i, (source, target) in enumerate(((q_hbm, q_ref), (k_hbm, k_ref), (v_hbm, v_ref)))
            ]
        )
        for read in reads[part]:
            read.start()
    left = lanes_left(rows)
    left24 = lanes_left(24)
    rate_scr[...] = jnp.zeros_like(rate_scr)
    rate_copy.wait()
    rate_scr[:, 0:rows] = r_ref[...].astype(f32)
    for part in range(parts):
        for read in reads[part]:
            read.wait()
        for p in range(each // 2 * part, each // 2 * (part + 1)):
            cols = slice(LANES * p, LANES * (p + 1))
            q = q_ref[:, cols].astype(f32)
            k = k_ref[:, cols].astype(f32)
            v = v_ref[:, cols].astype(f32)
            q_sw, k_sw, v_sw = swap_halves(q), swap_halves(k), swap_halves(v)
            for odd in (0, 1):
                head = 2 * p + odd
                qk = jnp.where(left, q_sw, k) if odd else jnp.where(left, q, k_sw)
                v_right, v_left = (v, v_sw) if odd else (v_sw, v)
                rate = jnp.broadcast_to(rate_scr[head : head + 1, :], (24 - late, LANES))
                low = jnp.concatenate([v_left[24:rows], rate], axis=0)
                vr = jnp.where(left24, low, v_right[0:24])
                o_ref[head] = jnp.concatenate([qk, vr], axis=0).astype(bf16)
        own = pl.ds(each * part, each)
        write = pltpu.make_async_copy(o_ref.at[own], o_hbm.at[own], out_sems.at[part])
        write.start()
        writes.append(write)
    for write in writes:
        write.wait()


def pack(queries, keys, values, rates_t):
    rows, width = queries.shape
    heads = width // HDIM
    return pl.pallas_call(
        pack_body,
        in_specs=[pl.BlockSpec(memory_space=pl.ANY)] * 4,
        out_specs=pl.BlockSpec(memory_space=pl.ANY),
        out_shape=jax.ShapeDtypeStruct((heads, rows + 24, LANES), bf16),
        scratch_shapes=[
            pltpu.VMEM((rows, width), bf16),
            pltpu.VMEM((rows, width), bf16),
            pltpu.VMEM((rows, width), bf16),
            pltpu.VMEM((heads, rows), bf16),
            pltpu.VMEM((heads, rows + 24, LANES), bf16),
            pltpu.VMEM((heads, LANES), f32),
            pltpu.SemaphoreType.DMA((PACK_PARTS, 4)),
            pltpu.SemaphoreType.DMA((PACK_PARTS,)),
        ],
        compiler_params=pltpu.CompilerParams(vmem_limit_bytes=PACK_LIMIT),
        name="pack",
    )(queries, keys, values, rates_t)


def packed(x):
    hi, lo = split(x)
    return jnp.where(lanes_left(x.shape[0]), hi.astype(f32), lo.astype(f32)).astype(bf16)


def twice(p):
    return jnp.concatenate([p, p], axis=1)


def four(hi, lo):
    return jnp.concatenate([hi, hi, lo, lo], axis=0)


def doubled_eye():
    row = lax.broadcasted_iota(jnp.int32, (HDIM, LANES), 0)
    col = lax.broadcasted_iota(jnp.int32, (HDIM, LANES), 1)
    return jnp.where(row == lax.rem(col, HDIM), 1.0, 0.0).astype(f32)


def norm_sums():
    row = lax.broadcasted_iota(jnp.int32, (2 * LANES, 2 * LANES), 0)
    col = lax.broadcasted_iota(jnp.int32, (2 * LANES, 2 * LANES), 1)
    is_key_row = lax.rem(row, LANES) >= HDIM
    return jnp.where(is_key_row == (col < LANES), 1.0, 0.0).astype(bf16)


def inverse_norms(qk, sums):
    hi, lo = split(qk * qk)
    return lax.rsqrt(mm(jnp.concatenate([hi, lo], axis=1), sums) + 1e-06)


def attend_body(
    tv_ref, me_ref, recv_ref, msg_ref, qk_ref, ar_ref, g_ref,
    qk_scr, v_scr, r_scr, inv_scr, rate_scr, k2_scr, qs_scr, tf_scr, tb_scr, da_scr, ckh_scr, ckl_scr, h_scr, reach_scr,
):
    groups, rows, _ = recv_ref.shape
    toks = rows - 24
    late = toks - 24
    seglen = groups * toks
    chunks = seglen // GROUP
    blocks = seglen // QROWS
    valid = tv_ref[0]
    me = me_ref[0]

    pick = lax.broadcasted_iota(jnp.int32, (toks, LANES), 0) == lax.broadcasted_iota(jnp.int32, (toks, LANES), 1)
    left24, left_late = lanes_left(24), lanes_left(late)
    for g in range(groups):
        block = recv_ref[g].astype(f32)
        base = toks * g
        qk_scr[base : base + toks] = block[0:toks]
        tail = block[toks : toks + 24]
        tail_sw = swap_halves(tail)
        v_scr[base : base + 24] = jnp.where(left24, tail_sw, tail)
        v_scr[base + 24 : base + toks] = jnp.where(left_late, tail[0:late], tail_sw[0:late])
        r_scr[base : base + toks] = jnp.where(pick, tail[late : late + 1], 0.0)

    sums = norm_sums()
    ones = jnp.ones((LANES, LANES), bf16)
    left = lanes_left(QROWS)

    for b in range(blocks):
        at = slice(QROWS * b, QROWS * (b + 1))
        inv_scr[at] = inverse_norms(qk_scr[at], sums)[:, 0:LANES]
        rate = mm(r_scr[at].astype(bf16), ones)
        if QROWS * b < TEXT:
            position = QROWS * b + lax.broadcasted_iota(jnp.int32, (QROWS, LANES), 0)
            rate = jnp.where((position >= TEXT) | (position < valid), rate, 0.0)
        rate_scr[at] = rate
    for b in range(blocks):
        at = slice(QROWS * b, QROWS * (b + 1))
        qk = qk_scr[at]
        kq = swap_halves(qk)
        k2 = jnp.where(left, kq, qk)
        k2_scr[at] = k2.astype(bf16)
        qk_ref[at] = qk.astype(bf16)
        qs_scr[at] = jnp.where(left, qk * (1.0 / math.sqrt(HDIM)), 0.0).astype(bf16)
        inv_k = inv_scr[at]
        step = rate_scr[at] * inv_k
        inv_scr[at] = step
        ck_hi, ck_lo = split(step * inv_k * k2)
        ckh_scr[at] = ck_hi
        ckl_scr[at] = ck_lo
    parts = seglen // AROWS
    cols = lax.broadcasted_iota(jnp.int32, (AROWS, TEXT), 1)
    left_part = lanes_left(AROWS)

    def scores_of(b):
        scores = mm_nt(qs_scr[AROWS * b : AROWS * (b + 1)], k2_scr[...])
        return jnp.concatenate([jnp.where(cols < valid, scores[:, 0:TEXT], -1e30), scores[:, TEXT:]], axis=1)

    scores = scores_of(0)
    for n in range(chunks):
        at = slice(GROUP * n, GROUP * (n + 1))
        k = k2_scr[at, 0:HDIM]
        gram = mm_tn(jnp.concatenate([k, k], axis=0), jnp.concatenate([ckh_scr[at], ckl_scr[at]], axis=0))
        g_hi, g_lo = split(gram)
        g_ref[n, 0:HDIM] = g_hi
        g_ref[n, HDIM : 2 * HDIM] = g_lo

    v2 = v_scr[...].astype(bf16)
    eye = doubled_eye()
    t_f, t_b = eye, eye

    def gram_right(n):
        return four(g_ref[n, 0:HDIM], g_ref[n, HDIM : 2 * HDIM])

    for m in range(chunks // 2):
        g0, g1 = (g_ref[2 * m + i, 0:HDIM].astype(f32) + g_ref[2 * m + i, HDIM : 2 * HDIM].astype(f32) for i in (0, 1))
        pair = g0 + g1 - mm(twice(packed(g0)), gram_right(2 * m + 1))
        hi, lo = split(pair)
        h_scr[m, 0:HDIM] = hi
        h_scr[m, HDIM : 2 * HDIM] = lo

    def advance_f(t, m):
        p = packed(t)
        keep(tf_scr, 2 * m, p)
        keep(tf_scr, 2 * m + 1, packed(t - mm(twice(p), gram_right(2 * m))))
        return t - mm(twice(p), four(h_scr[m, 0:HDIM], h_scr[m, HDIM : 2 * HDIM]))

    def advance_b(t, m):
        p = packed(t)
        keep(tb_scr, 2 * m + 1, p)
        keep(tb_scr, 2 * m, packed(t - mm(twice(p), gram_right(2 * m + 1))))
        hi, lo = h_scr[m, 0:HDIM], h_scr[m, HDIM : 2 * HDIM]
        row = jnp.concatenate([hi, lo], axis=1)
        return t - mm_nt(twice(p), jnp.concatenate([row, row], axis=0))

    def keep(ref, n, p):
        ref[GROUP * n : GROUP * (n + 1)] = p

    def close(b, raised, row_total):
        at = slice(AROWS * b, AROWS * (b + 1))
        att = (mm(raised, v2) / row_total).astype(bf16).astype(f32)
        ar_ref[at] = jnp.where(left_part, att, rate_scr[at]).astype(bf16)
        da_scr[at] = packed(inv_scr[at] * att)

    for b in range(parts):
        if b:
            close(b - 1, raised, row_total)
        following = scores_of(b + 1) if b + 1 < parts else None
        for m in range(chunks // 2 * b // parts, chunks // 2 * (b + 1) // parts):
            t_f = advance_f(t_f, m)
            t_b = advance_b(t_b, chunks // 2 - 1 - m)
        peak = jnp.max(scores, axis=1, keepdims=True)
        raised = jnp.exp(scores - peak)
        row_total = jnp.sum(raised, axis=1, keepdims=True)
        raised = raised.astype(bf16)
        scores = following
    close(parts - 1, raised, row_total)

    for n in range(chunks):
        at = slice(GROUP * n, GROUP * (n + 1))
        hi, lo = split(mm_nt(k2_scr[at], jnp.concatenate([tf_scr[at], tb_scr[at]], axis=0)))
        reach_scr[at] = jnp.concatenate([hi, lo], axis=1)
    total = mm_tn(da_scr[...], reach_scr[...])
    total = total[0:HDIM] + total[HDIM : 2 * HDIM]
    shift_f = total[:, 0:LANES] + total[:, LANES : 2 * LANES]
    shift_b = swap_halves(shift_f)
    left64 = lanes_left(HDIM)
    later = jnp.where(left64, t_f - eye, shift_f)
    earlier = jnp.where(left64, t_b - eye, shift_b)
    for s in range(msg_ref.shape[0]):
        msg_ref[s] = jnp.where(s > me, later, earlier).astype(msg_ref.dtype)


def attend(text_valid, me, received, segments, link):
    groups, rows, _ = received.shape
    seglen = groups * (rows - 24)
    chunks = seglen // GROUP
    smem = pl.BlockSpec(memory_space=pltpu.SMEM)
    vmem = pl.BlockSpec(memory_space=pltpu.VMEM)
    tall = (seglen, LANES)
    return pl.pallas_call(
        attend_body,
        in_specs=[smem, smem, vmem],
        out_specs=[vmem] * 4,
        out_shape=[jax.ShapeDtypeStruct((segments, HDIM, LANES), link)]
        + [jax.ShapeDtypeStruct(tall, bf16)] * 2
        + [jax.ShapeDtypeStruct((chunks, LANES, LANES), bf16)],
        scratch_shapes=[
            *[pltpu.VMEM(tall, f32)] * 5, *[pltpu.VMEM(tall, bf16)] * 7, pltpu.VMEM((chunks // 2, LANES, LANES), bf16),
            pltpu.VMEM((seglen, 2 * LANES), bf16),
        ],
        compiler_params=pltpu.CompilerParams(vmem_limit_bytes=VMEM_LIMIT),
        name="attend",
    )(text_valid, me, received)


def operators_body(
    qk_ref, ar_ref, g_ref, base_ref, ehi_ref, elo_ref,
    opf_scr, opb_scr, xf_scr, xb_scr, shift_scr, yhi_scr, ylo_scr, k2_scr, q2_scr, inv_scr,
):
    chunks = g_ref.shape[0]
    row_id = lax.broadcasted_iota(jnp.int32, (GROUP, LANES), 0)
    col_id = lax.rem(lax.broadcasted_iota(jnp.int32, (GROUP, LANES), 1), GROUP)
    left = lanes_left(GROUP)
    sums = norm_sums()
    eye = doubled_eye()
    x_f = jnp.concatenate([eye, jnp.zeros_like(eye)], axis=0)
    x_b = x_f

    def rows_of(n):
        return slice(GROUP * n, GROUP * (n + 1))

    def halves(x):
        x = x.astype(f32)
        x_sw = swap_halves(x)
        on_left = lanes_left(x.shape[0])
        return jnp.where(on_left, x, x_sw), jnp.where(on_left, x_sw, x)

    def advance(x, n, keep_ref):
        hi, lo = split(x)
        keep_ref[n] = jnp.concatenate([hi, lo], axis=1)
        p = jnp.where(lanes_left(2 * HDIM), hi.astype(f32), lo.astype(f32)).astype(bf16)
        x = x - mm(twice(p), four(g_ref[n, 0:HDIM], g_ref[n, HDIM : 2 * HDIM]))
        return jnp.concatenate([x[0:HDIM], x[HDIM : 2 * HDIM] + shift_scr[n]], axis=0)

    blocks = chunks * GROUP // QROWS
    for b in range(blocks):
        at = slice(QROWS * b, QROWS * (b + 1))
        inv_scr[at] = inverse_norms(qk_ref[at].astype(f32), sums)
    for b in range(blocks):
        at = slice(QROWS * b, QROWS * (b + 1))
        inv_k = inv_scr[at, 0:LANES]
        q2, k2 = halves(qk_ref[at])
        att, rate = halves(ar_ref[at])
        step = rate * inv_k
        ck_hi, ck_lo = split(step * inv_k * k2)
        da_hi, da_lo = split(step * att)
        yhi_scr[at] = jnp.concatenate([ck_hi, da_hi], axis=1)
        ylo_scr[at] = jnp.concatenate([ck_lo, da_lo], axis=1)
        base_ref[at] = att
        q2_scr[at] = q2.astype(bf16)
        k2_scr[at] = k2.astype(bf16)
    for n in range(chunks):
        at = rows_of(n)
        k2 = k2_scr[at]
        da = jnp.concatenate([yhi_scr[at, LANES : LANES + HDIM], ylo_scr[at, LANES : LANES + HDIM]], axis=0)
        shift_scr[n] = mm_tn(da, jnp.concatenate([k2, k2], axis=0))

    for n in range(chunks):
        x_f = advance(x_f, n, xf_scr)
        x_b = advance(x_b, chunks - 1 - n, xb_scr)
        at = rows_of(n)
        q2, k2 = q2_scr[at].astype(f32), k2_scr[at]
        scores = mm_nt(jnp.where(left, q2, 0.0).astype(bf16), jnp.concatenate([k2, k2], axis=0))
        both = packed(
            jnp.concatenate(
                [jnp.where(col_id <= row_id, scores, 0.0), jnp.where(col_id >= row_id, scores, 0.0)], axis=0
            )
        )
        y_hi, y_lo = yhi_scr[at], ylo_scr[at]
        pushed = mm(twice(both), four(y_hi, y_lo))
        scale = math.sqrt(HDIM) * inv_scr[at, LANES : 2 * LANES]
        opf_scr[at] = packed(scale * (q2 - pushed[0:GROUP, 0:LANES]))
        opb_scr[at] = packed(scale * (q2 - pushed[GROUP : 2 * GROUP, 0:LANES]))
        base_ref[at] = base_ref[at] + scale * (
            pushed[0:GROUP, LANES : 2 * LANES] + pushed[GROUP : 2 * GROUP, LANES : 2 * LANES]
        )

    for n in range(chunks):
        at = rows_of(n)

        def through(op_ref, x_ref):
            t, w = x_ref[n, 0:HDIM], x_ref[n, HDIM : 2 * HDIM]
            return mm_nt(twice(op_ref[at]), jnp.concatenate([t, t, w, w], axis=0))

        from_f, from_b = through(opf_scr, xf_scr), through(opb_scr, xb_scr)
        base_ref[at] = base_ref[at] + from_f[:, LANES : 2 * LANES] + from_b[:, LANES : 2 * LANES]
        e_hi, e_lo = split(jnp.where(left, from_f[:, 0:LANES], from_b[:, 0:LANES]))
        ehi_ref[at] = e_hi
        elo_ref[at] = e_lo


def operators(*held):
    tall = held[0].shape
    chunks = tall[0] // GROUP
    state = (chunks, 2 * HDIM, 2 * LANES)
    return pl.pallas_call(
        operators_body,
        out_shape=[
            jax.ShapeDtypeStruct(tall, f32),
            jax.ShapeDtypeStruct(tall, bf16),
            jax.ShapeDtypeStruct(tall, bf16),
        ],
        scratch_shapes=[
            pltpu.VMEM(tall, bf16), pltpu.VMEM(tall, bf16), pltpu.VMEM(state, bf16), pltpu.VMEM(state, bf16),
            pltpu.VMEM((chunks, HDIM, LANES), f32),
            pltpu.VMEM((tall[0], 2 * LANES), bf16), pltpu.VMEM((tall[0], 2 * LANES), bf16),
            pltpu.VMEM(tall, bf16), pltpu.VMEM(tall, bf16), pltpu.VMEM((tall[0], 2 * LANES), f32),
        ],
        compiler_params=pltpu.CompilerParams(vmem_limit_bytes=VMEM_LIMIT),
        cost_estimate=pl.CostEstimate(flops=2_000_000_000, bytes_accessed=8_000_000, transcendentals=0),
        name="operators",
    )(*held)


def finish_body(me_ref, msg_ref, sf_ref, sb_ref, base_ref, ehi_ref, elo_ref, out_ref):
    segments = msg_ref.shape[0]
    groups, quad, wide = out_ref.shape
    half = quad * wide // LANES
    me = me_ref[0]
    left64 = lanes_left(HDIM)

    def doubled_transpose(state):
        return jnp.concatenate([state, state], axis=0).T

    def times(x, decay):
        return mm(twice(packed(x)), four(*split(decay)))

    def times_sent(x, decay):
        decay = decay.astype(bf16)
        return mm(packed(x), jnp.concatenate([decay, decay], axis=0))

    def leaf(i):
        m = msg_ref[i].astype(f32)
        m_sw = swap_halves(m)
        return jnp.concatenate([jnp.where(left64, m, m_sw), jnp.where(left64, m_sw, m)], axis=0)

    def then(first, second, times):
        return first + second + times(first, second[0:HDIM])

    def sibling(level):
        size = 2**level
        block = lax.div(me, size)
        before = lax.rem(block, 2) == 1
        start = jnp.where(before, block - 1, block + 1) * size
        nodes = [leaf(start + jnp.where(before, i, size - 1 - i)) for i in range(size)]
        way = times_sent
        while len(nodes) > 1:
            nodes = [then(nodes[i], nodes[i + 1], way) for i in range(0, len(nodes), 2)]
            way = times
        return before, nodes[0], way

    w_f, w_b = doubled_transpose(sf_ref[0]), doubled_transpose(sb_ref[0])
    for before, node, way in [sibling(level) for level in reversed(range(segments.bit_length() - 1))]:
        state = jnp.where(before, w_f, w_b)
        state = state + way(state, node[0:HDIM]) + node[HDIM : 2 * HDIM]
        w_f, w_b = jnp.where(before, state, w_f), jnp.where(before, w_b, state)
    w_hi, w_lo = split(jnp.where(left64, w_f, w_b))
    w_row = jnp.concatenate([w_hi, w_hi, w_lo], axis=1)
    e_hi = ehi_ref[...]
    got = mm_nt(jnp.concatenate([e_hi, elo_ref[...], e_hi], axis=1), jnp.concatenate([w_row, w_row], axis=0))
    whole = got + base_ref[...]
    left = lanes_left(2 * quad)
    for g in range(groups):
        for j in range(wide // LANES):
            row = 2 * half * g + 2 * quad * j
            rows = whole[row : row + 2 * quad]
            both = jnp.where(left, rows, pltpu.roll(rows, quad, 0))
            out_ref[g, :, LANES * j : LANES * (j + 1)] = both[0:quad].astype(bf16)


def finish(me, maps, state_fwd, state_bwd, base, ehi, elo, groups):
    seglen = base.shape[0]
    half = seglen // groups // 2
    smem = pl.BlockSpec(memory_space=pltpu.SMEM)
    vmem = pl.BlockSpec(memory_space=pltpu.VMEM)
    return pl.pallas_call(
        finish_body,
        in_specs=[smem] + [vmem] * 6,
        out_specs=vmem,
        out_shape=jax.ShapeDtypeStruct((groups, QUAD, half // QUAD * LANES), bf16),
        compiler_params=pltpu.CompilerParams(vmem_limit_bytes=VMEM_LIMIT),
        name="finish",
    )(me, maps, state_fwd, state_bwd, base, ehi, elo)


def unpack_body(x_ref, out_ref, scr, rows_scr):
    heads, quad, wide = x_ref.shape
    half = quad * wide // LANES
    left = lanes_left(half)
    for head in range(heads):
        for j in range(wide // LANES):
            rows_scr[head, quad * j : quad * (j + 1)] = x_ref[head, :, LANES * j : LANES * (j + 1)].astype(f32)
    for p in range(heads // 2):
        even = rows_scr[2 * p]
        odd = rows_scr[2 * p + 1]
        first = jnp.where(left, even, swap_halves(odd))
        second = jnp.where(left, swap_halves(even), odd)
        for j in range(wide // LANES):
            scr[p, 2 * quad * j : 2 * quad * j + quad] = first[quad * j : quad * (j + 1)]
            scr[p, 2 * quad * j + quad : 2 * quad * (j + 1)] = second[quad * j : quad * (j + 1)]
    for p in range(heads // 2):
        out_ref[:, LANES * p : LANES * (p + 1)] = scr[p].astype(bf16)


def unpack(x):
    heads, quad, wide = x.shape
    half = quad * wide // LANES
    return pl.pallas_call(
        unpack_body,
        out_shape=jax.ShapeDtypeStruct((2 * half, heads * HDIM), bf16),
        scratch_shapes=[pltpu.VMEM((heads // 2, 2 * half, LANES), f32), pltpu.VMEM((heads, half, LANES), f32)],
        compiler_params=pltpu.CompilerParams(vmem_limit_bytes=VMEM_LIMIT),
        name="unpack",
    )(x)


def exchange(x, axis):
    return lax.all_to_all(x, axis, split_axis=0, concat_axis=0, tiled=True)


def local(queries, keys, values, rates, text_valid, state_fwd, state_bwd):
    segments = lax.axis_size("seg")
    groups = lax.axis_size("grp")
    me = lax.axis_index("seg").astype(jnp.int32).reshape(1)
    received = exchange(pack(queries, keys, values, rates.T), "grp")
    msg, *held = attend(text_valid, me, received, segments, bf16)
    maps = exchange(msg, "seg")
    base, ehi, elo = operators(*held)
    mixed = finish(me, maps, state_fwd, state_bwd, base, ehi, elo, groups)
    return unpack(exchange(mixed, "grp"))


def solution(mesh):
    in_specs = (
        P(("seg", "grp"), None),
        P(("seg", "grp"), None),
        P(("seg", "grp"), None),
        P(("seg", "grp"), None),
        P("seg"),
        P("grp", None, None),
        P("grp", None, None),
    )
    out_specs = P(("seg", "grp"), None)
    return jax.shard_map(local, mesh=mesh, in_specs=in_specs, out_specs=out_specs, check_vma=False)
```
